512 devices in a mesh: gx: 8 (over y), gy: 16 (over z, core), lev: 4 (over x).
Axes of the slice: x: 4, y: 8, z: 8, core: 2. Of those that a mesh axis runs over, the one named last changes fastest.
Arguments:
- wind_x: float32 [128, 256, 2048], P('lev', 'gx', 'gy'), may hold values from -6 to 6
- wind_y: float32 [128, 256, 2048], P('lev', 'gx', 'gy'), may hold values from -6 to 6
- wind_z: float32 [128, 256, 2048], P('lev', 'gx', 'gy'), may hold values from -6 to 6
- pressure: float32 [128, 256, 2048], P('lev', 'gx', 'gy'), may hold values from -6 to 6
- jacobian: float32 [256, 2048], P('gx', 'gy'), may hold values from 0.5 to 2
- slope_x: float32 [256, 2048], P('gx', 'gy'), may hold values from -3 to 3
- slope_y: float32 [256, 2048], P('gx', 'gy'), may hold values from -3 to 3
- stiffness: float32 [128, 256, 2048], P('lev', 'gx', 'gy'), may hold values from 10 to 1000
Outputs:
- wind_x_out: float32 [128, 256, 2048], P('lev', 'gx', 'gy')
- wind_y_out: float32 [128, 256, 2048], P('lev', 'gx', 'gy')
- wind_z_out: float32 [128, 256, 2048], P('lev', 'gx', 'gy')
- pressure_out: float32 [128, 256, 2048], P('lev', 'gx', 'gy')
The draws below stay inside these ranges and needn't reach their ends.
All inputs are finite; a program needn't handle non-finite values.
Results may differ from the reference program's by a relative error of at most 0.000096.
Values sent between devices are 32-bit elements; how exact they have to be, the bound alone decides.
A program may use at most 64 MiB of HBM per device.

```python
import math
import jax
import jax.numpy as jnp
from jax import lax

SUBSTEPS = 2
NX = 256
NY = 2048
NZ = 128


def steps_of(key, extent, cuts, least, high):
    gain = 1.0
    for position, parts in cuts:
        draws = jax.random.uniform(jax.random.fold_in(jax.random.fold_in(key, 6), position), (parts,), jnp.float32, least / len(cuts), high / len(cuts))
        gain = gain * jnp.repeat(jnp.exp(draws), extent[position] // parts).reshape((-1,) + (1,) * (len(extent) - 1 - position))
    return gain


def centred(rng, dims, width, bound, shards=(), dtype=jnp.bfloat16):
    array = width * jax.random.normal(rng, dims, jnp.float32)
    if shards:
        array = array * steps_of(rng, dims, shards, -0.22, 0.18)
    return jnp.clip(array, -bound, bound).astype(dtype)


def setup_inputs(seed: int = 0) -> dict:
    splits = jax.random.split(jax.random.key(seed), 9)
    return {
        "wind_x": centred(splits[0], (NZ, NX, NY), 1.0, 6.0, ((0, 4), (1, 8), (2, 16)), jnp.float32),
        "wind_y": centred(splits[1], (NZ, NX, NY), 1.0, 6.0, ((0, 4), (1, 8), (2, 16)), jnp.float32),
        "wind_z": centred(splits[2], (NZ, NX, NY), 1.0, 6.0, ((0, 4), (1, 8), (2, 16)), jnp.float32),
        "pressure": centred(splits[3], (NZ, NX, NY), 1.0, 6.0, ((0, 4), (1, 8), (2, 16)), jnp.float32),
        "jacobian": jnp.clip(jnp.exp(math.log(2.0) - 1.3862944 * jax.random.uniform(splits[4], (NX, NY), jnp.float32) ** steps_of(splits[4], (NX, NY), ((0, 8), (1, 16)), -0.2, 0.2)), 0.5, 2.0),
        "slope_x": centred(splits[5], (NX, NY), 0.5, 3.0, ((0, 8), (1, 16)), jnp.float32),
        "slope_y": centred(splits[6], (NX, NY), 0.5, 3.0, ((0, 8), (1, 16)), jnp.float32),
        "stiffness": jnp.clip(jnp.exp(math.log(1000.0) - 4.6051702 * jax.random.uniform(splits[7], (NZ, NX, NY), jnp.float32) ** steps_of(splits[7], (NZ, NX, NY), ((0, 4), (1, 8), (2, 16)), -0.2, 0.2)), 10.0, 1000.0),
    }


grad_coef = 0.35
div_coef = 0.35
vert_coef = 0.25


def diff_four(field, axis):
    return (jnp.roll(field, 2, axis) - 8.0 * jnp.roll(field, 1, axis) + 8.0 * jnp.roll(field, -1, axis) - jnp.roll(field, -2, axis)) / 12.0


def vert_diff(field):
    padded = jnp.pad(field, ((1, 1), (0, 0), (0, 0)))
    return padded[2:] - padded[:-2]


def column_thomas(stiffness, source):
    def forward(carry, level):
        ratio, value = carry
        coef, rhs = level
        denom = 1.0 + 2.0 * coef + coef * ratio
        new_ratio = -coef / denom
        new_value = (rhs + coef * value) / denom
        return (new_ratio, new_value), (new_ratio, new_value)

    start = jnp.zeros(source.shape[1:], jnp.float32)
    _, (ratios, values) = lax.scan(forward, (start, start), (stiffness, source))

    def backward(upper, level):
        ratio, value = level
        result = value - ratio * upper
        return result, result

    _, solved = lax.scan(backward, start, (ratios, values), reverse=True)
    return solved


def reference(wind_x, wind_y, wind_z, pressure, jacobian, slope_x, slope_y, stiffness):
    for substep in range(SUBSTEPS):
        new_x = wind_x - grad_coef * diff_four(pressure, 1)
        new_y = wind_y - grad_coef * diff_four(pressure, 2)
        divergence = (diff_four(jacobian * new_x, 1) + diff_four(jacobian * new_y, 2)) / jacobian
        pres_star = pressure - div_coef * divergence
        source = wind_z + slope_x * new_x + slope_y * new_y - vert_coef * vert_diff(pres_star)
        wind_z = column_thomas(stiffness, source)
        pressure = pres_star - vert_coef * vert_diff(wind_z)
        wind_x, wind_y = new_x, new_y
    return (wind_x, wind_y, wind_z, pressure)
```

```python
import jax
import jax.numpy as jnp
from jax import lax
from jax.experimental import pallas as pl
from jax.experimental.pallas import tpu as pltpu
from jax.sharding import PartitionSpec as P

SUBSTEPS = 2
GRAD = 0.35 / 12.0
VERT = 0.25

NZ, NX, NY = 32, 32, 128
GAP = 8
WIDE = NX + 2 * GAP
LEVS = 4
UNROLL = 4
F32 = jnp.float32


def level_rows(ref, row, first=0):
    levels, rows, lanes = ref.shape
    return ref.reshape(levels * rows, lanes), pl.ds(first * rows + row, NZ, stride=rows)


def get_rows(ref, row, first=0):
    flat, there = level_rows(ref, row, first)
    return flat[there, :]


def set_rows(ref, row, value, first=0):
    flat, there = level_rows(ref, row, first)
    flat[there, :] = value


def kernel(
    wx_h, wy_h, wz_h, p_h, j_h, sx_h, sy_h, st_h,
    ox_h, oy_h, oz_h, op_h,
    pbuf, fbuf, wx, wy, wz, ps, st, inv, up_s, q_s, val,
    jac, ijac, slx, sly,
    wyp, npk, jpk, ijpk, nrow,
    ymsg, xmsg, yrecv, xrecv, jprecv, jrecv, strecv,
    vset, vsetrecv, vmsg, vrecv, coef,
    load_sem, store_sem,
    hs_send, hs_recv, ss_send, ss_recv, vs_send, vs_recv, js_send, js_recv, es_send, es_recv,
):
    gx, gy, lev = lax.axis_index("gx"), lax.axis_index("gy"), lax.axis_index("lev")
    ngx, ngy = lax.axis_size("gx"), lax.axis_size("gy")
    xlo, xhi = lax.rem(gx + ngx - 1, ngx), lax.rem(gx + 1, ngx)
    ylo, yhi = lax.rem(gy + ngy - 1, ngy), lax.rem(gy + 1, ngy)
    up, down, over = lax.rem(lev + 1, LEVS), lax.rem(lev + 3, LEVS), lax.rem(lev + 2, LEVS)
    mesh_id = pl.DeviceIdType.MESH

    def remote(src, dst, send, recv, where):
        return pltpu.make_async_remote_copy(
            src_ref=src, dst_ref=dst, send_sem=send, recv_sem=recv,
            device_id=where, device_id_type=mesh_id,
        )

    loads = [
        pltpu.make_async_copy(src, dst, load_sem.at[i])
        for i, (src, dst) in enumerate((
            (p_h, pbuf.at[:, GAP:GAP + NX, :]), (wy_h, wy), (wx_h, wx), (j_h, jac),
            (st_h, st), (sx_h, slx), (sy_h, sly), (wz_h, wz),
        ))
    ]
    for copy in loads:
        copy.start()
    barrier = pltpu.get_barrier_semaphore()
    partners = (
        {"gx": xlo}, {"gx": xhi}, {"gy": ylo}, {"gy": yhi},
        {"lev": up}, {"lev": down}, {"lev": over},
    )
    for where in partners:
        pl.semaphore_signal(barrier, inc=1, device_id=where, device_id_type=mesh_id)

    gap = jnp.zeros((GAP, NY), F32)

    def clear(l, carry):
        pbuf[l, 0:GAP, :] = gap
        pbuf[l, GAP + NX:WIDE, :] = gap
        fbuf[l, 0:GAP, :] = gap
        fbuf[l, GAP + NX:WIDE, :] = gap
        return carry

    lax.fori_loop(0, NZ, clear, 0, unroll=UNROLL)
    ps[0] = jnp.zeros((NX, NY), F32)
    ps[NZ + 1] = jnp.zeros((NX, NY), F32)

    lane = lax.broadcasted_iota(jnp.int32, (1, NY), 1)
    pos, group = lane & 7, lane >> 3

    def at(value, *places):
        hit = pos == places[0]
        for place in places[1:]:
            hit = hit | (pos == place)
        return jnp.where(hit, F32(value), F32(0))

    own_taps = (
        (2, at(1.0, 2, 3, 6, 7)), (1, at(-8.0, 1, 2, 3, 5, 6, 7)),
        (NY - 1, at(8.0, 0, 1, 2, 4, 5, 6)), (NY - 2, at(-1.0, 0, 1, 4, 5)),
    )
    far_taps = (
        (2, at(1.0, 4, 5)), (1, at(-8.0, 4)), (NY - 1, at(8.0, 3)), (NY - 2, at(-1.0, 2, 3)),
    )

    def taps(z, which):
        return sum(c * pltpu.roll(z, s, 1) for s, c in which)

    low_half, inner = pos < 4, (pos >= 2) & (pos <= 5)
    near_edge = (lane < 4) | (lane >= NY - 4)

    def lane_taps(scale):
        return (
            (2, jnp.where(lane >= 2, F32(scale), F32(0))),
            (1, jnp.where(lane >= 1, F32(-8.0 * scale), F32(0))),
            (NY - 1, jnp.where(lane < NY - 1, F32(8.0 * scale), F32(0))),
            (NY - 2, jnp.where(lane < NY - 2, F32(-scale), F32(0))),
        )

    grad_taps, unit_taps = lane_taps(-GRAD), lane_taps(1.0)

    loads[0].wait()
    loads[1].wait()
    acc0 = jnp.zeros((NX, NY), F32)
    for half in range(2):
        def pack(i, carry):
            a, b = carry
            here = group == i
            l = half * 16 + i
            a = jnp.where(here, pltpu.roll(pbuf[l, GAP:GAP + NX, :], 8 * i + 4, 1), a)
            b = jnp.where(here, pltpu.roll(wy[l], (8 * i + 4) , 1), b)
            return a, b

        a, b = lax.fori_loop(0, 15, pack, (acc0, acc0), unroll=5)
        here = group == 15
        a = jnp.where(here, pltpu.roll(pbuf[half * 16 + 15, GAP:GAP + NX, :], 124, 1), a)
        b = jnp.where(here, pltpu.roll(wy[half * 16 + 15], 124, 1), b)
        ymsg[half] = a
        wyp[half] = b

    loads[3].wait()
    j = jac[...]
    ijac[...] = 1.0 / j
    z = jnp.where(lane < 8, pltpu.roll(j, 4, 1), 0.0)
    for shift in (8, 16, 32, 64):
        z = z + pltpu.roll(z, shift, 1)
    jpk[...] = z
    ijpk[...] = 1.0 / z
    loads[2].wait()

    def prow(r):
        return get_rows(pbuf, GAP + r)

    def jrow(r):
        return jac[r:r + 1, :]

    def y_copies(step):
        return (
            remote(ymsg.at[2:4], yrecv.at[step, 0], hs_send.at[0], hs_recv.at[step, 0], {"gy": yhi}),
            remote(ymsg.at[2:4], yrecv.at[step, 1], hs_send.at[1], hs_recv.at[step, 1], {"gy": ylo}),
        )

    def x_copies(step):
        return (
            remote(xmsg.at[1], xrecv.at[step, 0], hs_send.at[2], hs_recv.at[step, 2], {"gx": xhi}),
            remote(xmsg.at[0], xrecv.at[step, 1], hs_send.at[3], hs_recv.at[step, 3], {"gx": xlo}),
        )

    def edges_out(step):
        p0, p1, p2, p3 = (prow(r) for r in range(4))
        p28, p29, p30, p31 = (prow(r) for r in range(NX - 4, NX))
        n0 = get_rows(wx, 0) - GRAD * (8.0 * p1 - p2)
        n1 = get_rows(wx, 1) - GRAD * (8.0 * (p2 - p0) - p3)
        n30 = get_rows(wx, NX - 2) - GRAD * (p28 + 8.0 * (p31 - p29))
        n31 = get_rows(wx, NX - 1) - GRAD * (p29 - 8.0 * p30)
        for i, n in enumerate((n0, n1, n30, n31)):
            nrow[i] = n
        xmsg[0, 0] = p0
        xmsg[0, 1] = p1
        xmsg[0, 2] = jrow(0) * n0
        xmsg[0, 3] = jrow(1) * n1
        xmsg[1, 0] = p30
        xmsg[1, 1] = p31
        xmsg[1, 2] = jrow(NX - 2) * n30
        xmsg[1, 3] = jrow(NX - 1) * n31
        if step == 0:
            pl.semaphore_wait(barrier, len(partners))
        for copy in x_copies(step):
            copy.start()
        jp = jpk[...]
        for half in range(2):
            pp = ymsg[half]
            n = wyp[half] - GRAD * taps(pp, own_taps)
            npk[half] = n
            flux = jp * n
            far = jnp.where(pos < 2, pltpu.roll(flux, NY - 2, 1), pltpu.roll(flux, 2, 1))
            ymsg[2 + half] = jnp.where(inner, pp, far)
        for copy in y_copies(step):
            copy.start()

    def edges_in(step):
        for copy in x_copies(step):
            copy.wait()
        p0, p1, p30, p31 = (xmsg[0, 0], xmsg[0, 1], xmsg[1, 0], xmsg[1, 1])
        low, high = xrecv.at[step, 0], xrecv.at[step, 1]
        jm2, jm1 = jrecv[0, 6:7, :], jrecv[0, 7:8, :]
        j32, j33 = jrecv[1, 0:1, :], jrecv[1, 1:2, :]
        pm2, pm1, p32, p33 = low[0], low[1], high[0], high[1]
        d0 = -GRAD * (pm2 - 8.0 * pm1)
        d1 = -GRAD * pm1
        d30 = GRAD * p32
        d31 = -GRAD * (8.0 * p32 - p33)
        fm2 = low[2] + (GRAD * jm2) * p0
        fm1 = low[3] - (GRAD * jm1) * (8.0 * p0 - p1)
        f32 = high[2] - (GRAD * j32) * (p30 - 8.0 * p31)
        f33 = high[3] - (GRAD * j33) * p31
        g0, g1 = jrow(0) * d0, jrow(1) * d1
        g30, g31 = jrow(NX - 2) * d30, jrow(NX - 1) * d31
        for i, (r, d) in enumerate(((0, d0), (1, d1), (NX - 2, d30), (NX - 1, d31))):
            set_rows(wx, r, nrow[i] + d)
        sums = (
            (0, fm2 + 8.0 * (g1 - fm1)), (1, fm1 - 8.0 * g0), (2, g0 - 8.0 * g1), (3, g1),
            (NX - 4, -g30), (NX - 3, 8.0 * g30 - g31), (NX - 2, 8.0 * g31 - f32),
            (NX - 1, 8.0 * (f32 - g30) - f33),
        )
        for r, s in sums:
            set_rows(ps, r, get_rows(ps, r, 1) - (GRAD * ijac[r:r + 1, :]) * s, 1)

        for copy in y_copies(step):
            copy.wait()
        jp, ijp = jpk[...], ijpk[...]
        jh = jnp.where(low_half, jprecv[0], jprecv[1])
        for half in range(2):
            m = jnp.where(low_half, yrecv[step, 0, half], yrecv[step, 1, half])
            pp = ymsg[half]
            d = -GRAD * taps(m, far_taps)
            part = jnp.where(low_half, pltpu.roll(m, 2, 1), pltpu.roll(m, NY - 2, 1))
            fh = part - GRAD * jh * taps(pp, far_taps)
            s = taps(jp * d, own_taps) + taps(fh, far_taps)
            wyp[half] = npk[half] + d
            dp = (-GRAD) * ijp * s

            def unpack(i, carry):
                l = half * 16 + i
                shift = lax.rem(124 - 8 * i + NY, NY)
                wy[l] = wy[l] + jnp.where(near_edge, pltpu.roll(d, shift, 1), 0.0)
                ps[l + 1] = ps[l + 1] + jnp.where(near_edge, pltpu.roll(dp, shift, 1), 0.0)
                return carry

            lax.fori_loop(0, 16, unpack, 0, unroll=UNROLL)

    def local_step():
        def gradients(l, carry):
            p = pbuf[l, GAP:GAP + NX, :]
            dx = (pbuf[l, GAP - 2:GAP + NX - 2, :] - pbuf[l, GAP + 2:GAP + NX + 2, :]) + 8.0 * (
                pbuf[l, GAP + 1:GAP + NX + 1, :] - pbuf[l, GAP - 1:GAP + NX - 1, :])
            nx = wx[l] - GRAD * dx
            wx[l] = nx
            fbuf[l, GAP:GAP + NX, :] = jac[...] * nx
            wy[l] = wy[l] + taps(p, grad_taps)
            return carry

        lax.fori_loop(0, NZ, gradients, 0, unroll=UNROLL)

        def divergence(l, carry):
            dx = (fbuf[l, GAP - 2:GAP + NX - 2, :] - fbuf[l, GAP + 2:GAP + NX + 2, :]) + 8.0 * (
                fbuf[l, GAP + 1:GAP + NX + 1, :] - fbuf[l, GAP - 1:GAP + NX - 1, :])
            dy = taps(jac[...] * wy[l], unit_taps)
            ps[l + 1] = pbuf[l, GAP:GAP + NX, :] - (GRAD * ijac[...]) * (dx + dy)
            return carry

        lax.fori_loop(0, NZ, divergence, 0, unroll=UNROLL)

    jac_copies = (
        remote(jpk, jprecv.at[0], js_send.at[0], js_recv.at[0], {"gy": yhi}),
        remote(jpk, jprecv.at[1], js_send.at[1], js_recv.at[1], {"gy": ylo}),
        remote(jac.at[NX - 8:NX], jrecv.at[0], js_send.at[2], js_recv.at[2], {"gx": xhi}),
        remote(jac.at[0:8], jrecv.at[1], js_send.at[3], js_recv.at[3], {"gx": xlo}),
    )
    stiff_copies = (
        remote(st.at[NZ - 1], strecv.at[0], es_send.at[0], es_recv.at[0], {"lev": up}),
        remote(st.at[0], strecv.at[1], es_send.at[1], es_recv.at[1], {"lev": down}),
    )
    set_copies = (
        remote(vset, vsetrecv.at[lev], ss_send.at[0], ss_recv.at[0], {"lev": up}),
        remote(vset, vsetrecv.at[lev], ss_send.at[1], ss_recv.at[1], {"lev": down}),
        remote(vset, vsetrecv.at[lev], ss_send.at[2], ss_recv.at[2], {"lev": over}),
    )
    set_arrivals = (
        remote(vset, vsetrecv.at[down], ss_send.at[0], ss_recv.at[0], {"lev": up}),
        remote(vset, vsetrecv.at[up], ss_send.at[1], ss_recv.at[1], {"lev": down}),
        remote(vset, vsetrecv.at[over], ss_send.at[2], ss_recv.at[2], {"lev": over}),
    )

    def v_copies(step, arrivals):
        a, b, c = (down, up, over) if arrivals else (lev, lev, lev)
        return (
            remote(vmsg.at[1:4], vrecv.at[step, a, 1:4], vs_send.at[0], vs_recv.at[step, 0], {"lev": up}),
            remote(vmsg.at[0:3], vrecv.at[step, b, 0:3], vs_send.at[1], vs_recv.at[step, 1], {"lev": down}),
            remote(vmsg.at[1:3], vrecv.at[step, c, 1:3], vs_send.at[2], vs_recv.at[step, 2], {"lev": over}),
        )

    edges_out(0)
    for copy in jac_copies:
        copy.start()
    loads[4].wait()
    for copy in stiff_copies:
        copy.start()

    def factor(i, carry):
        rising, falling = carry
        h = NZ - 1 - i
        inv_l, inv_h = 1.0 / st[i], 1.0 / st[h]
        rising = 1.0 / (2.0 + inv_l - rising)
        falling = 1.0 / (2.0 + inv_h - falling)
        up_s[i] = rising
        val[h] = falling
        return rising, falling

    lax.fori_loop(0, NZ, factor, (acc0, acc0), unroll=UNROLL)

    def spikes(i, carry):
        below, above = carry
        h = NZ - 1 - i
        below = below * val[i]
        above = above * up_s[h]
        val[i] = below
        q_s[h] = above
        inv[i] = 1.0 / st[i]
        return below, above

    ones = jnp.ones((NX, NY), F32)
    lax.fori_loop(0, NZ, spikes, (ones, ones), unroll=UNROLL)
    p_s = st
    vset[0] = val[0]
    vset[1] = q_s[0]
    vset[2] = q_s[NZ - 1]
    for copy in set_copies:
        copy.start()
    for copy in stiff_copies:
        copy.wait()

    def keep(l, carry):
        p_s[l] = val[l]
        return carry

    lax.fori_loop(0, NZ, keep, 0, unroll=UNROLL)

    def after_setup():
        for copy in set_copies:
            copy.wait_send()
        for copy in set_arrivals:
            copy.wait_recv()
        vsetrecv[lev] = vset[...]
        pa = [vsetrecv[i, 0] for i in range(LEVS)]
        qa = [vsetrecv[i, 1] for i in range(LEVS)]
        qb = [vsetrecv[i, 2] for i in range(LEVS)]
        b0 = qb[0]
        t1 = qa[1] / (1.0 - b0 * pa[1])
        b1 = qb[1] + t1 * b0 * qa[1]
        t2 = qa[2] / (1.0 - b1 * pa[2])
        b2 = qb[2] + t2 * b1 * qa[2]
        e3 = pa[3]
        r2 = qa[2] / (1.0 - e3 * qb[2])
        e2 = pa[2] + r2 * e3 * qa[2]
        r1 = qa[1] / (1.0 - e2 * qb[1])
        e1 = pa[1] + r1 * e2 * qa[1]
        z0 = 1.0 / (1.0 - b0 * e1)
        z1 = 1.0 / (1.0 - b1 * e2)
        z2 = 1.0 / (1.0 - b2 * e3)
        for i, c in enumerate((t1, b0, b1, t2, r1, r2, e2, e3, e1, b2, z0, z1, z2)):
            coef[i] = c
        coef[13] = 1.0 / strecv[0]
        coef[14] = 1.0 / strecv[1]

    def pick(*values):
        out = values[-1]
        for i in range(LEVS - 2, -1, -1):
            out = jnp.where(lev == i, values[i], out)
        return out

    for step in range(SUBSTEPS):
        last = step == SUBSTEPS - 1
        if step > 0:
            edges_out(step)
        local_step()
        if step == 0:
            for copy in jac_copies:
                copy.wait()
        edges_in(step)
        if last:
            out_x = pltpu.make_async_copy(wx, ox_h, store_sem.at[0])
            out_y = pltpu.make_async_copy(wy, oy_h, store_sem.at[1])
            out_x.start()
            out_y.start()
        if step == 0:
            for copy in loads[5:]:
                copy.wait()
            after_setup()

        def rising(l, carry):
            v, total = carry
            rhs = wz[l] + slx[...] * wx[l] + sly[...] * wy[l] - VERT * (ps[l + 2] - ps[l])
            rhs = rhs * inv[l]
            total = total + p_s[l] * rhs
            v = (rhs + v) * up_s[l]
            val[l] = v
            return v, total

        top, bottom = lax.fori_loop(0, NZ, rising, (acc0, acc0), unroll=UNROLL)
        vmsg[0] = ps[1]
        vmsg[1] = bottom - VERT * ps[1] * coef[13]
        vmsg[2] = top + VERT * ps[NZ] * coef[14]
        vmsg[3] = ps[NZ]
        for copy in v_copies(step, False):
            copy.start()

        def falling(i, x):
            l = NZ - 2 - i
            x = val[l] + up_s[l] * x
            val[l] = x
            return x

        lax.fori_loop(0, NZ - 1, falling, top, unroll=UNROLL)

        for copy in v_copies(step, False):
            copy.wait_send()
        for copy in v_copies(step, True):
            copy.wait_recv()
        vrecv[step, lev] = vmsg[...]
        ga = [vrecv[step, i, 1] for i in range(LEVS)]
        gb = [vrecv[step, i, 2] for i in range(LEVS)]
        t1, b0, b1, t2, r1, r2, e2, e3, e1, b2, z0, z1, z2 = (coef[i] for i in range(13))
        a0 = gb[0]
        a1 = gb[1] + t1 * (a0 + b0 * ga[1])
        a2 = gb[2] + t2 * (a1 + b1 * ga[2])
        c3 = ga[3]
        c2 = ga[2] + r2 * (c3 + e3 * gb[2])
        c1 = ga[1] + r1 * (c2 + e2 * gb[1])
        w = pick(acc0, (a0 + b0 * c1) * z0, (a1 + b1 * c2) * z1, (a2 + b2 * c3) * z2)
        y = pick((c1 + e1 * a0) * z0, (c2 + e2 * a1) * z1, (c3 + e3 * a2) * z2, acc0)
        under = jnp.where(lev == 0, acc0, w - VERT * vrecv[step, down, 3] * inv[0])
        above = jnp.where(lev == LEVS - 1, acc0, y + VERT * vrecv[step, up, 0] * inv[NZ - 1])

        def solved(l):
            return val[l] + p_s[l] * w + q_s[l] * y

        first = solved(0)
        for half in range(2):
            def finish(i, carry):
                before, here, packed = carry
                l = half * 16 + i
                after = solved(l + 1)
                wz[l] = here
                p = ps[l + 1] - VERT * (after - before)
                pbuf[l, GAP:GAP + NX, :] = p
                if not last:
                    packed = jnp.where(group == i, pltpu.roll(p, lax.rem(8 * i + 4, NY), 1), packed)
                return here, after, packed

            if half == 0:
                carry = lax.fori_loop(0, 16, finish, (under, first, acc0), unroll=UNROLL)
                ymsg[0] = carry[2]
            else:
                before, here, packed = lax.fori_loop(0, 15, finish, (carry[0], carry[1], acc0), unroll=5)
                wz[NZ - 1] = here
                p = ps[NZ] - VERT * (above - before)
                pbuf[NZ - 1, GAP:GAP + NX, :] = p
                ymsg[1] = jnp.where(group == 15, pltpu.roll(p, 124, 1), packed)
    out_z = pltpu.make_async_copy(wz, oz_h, store_sem.at[2])
    out_p = pltpu.make_async_copy(pbuf.at[:, GAP:GAP + NX, :], op_h, store_sem.at[3])
    out_z.start()
    out_p.start()
    out_x.wait()
    out_y.wait()
    out_z.wait()
    out_p.wait()


def local(*blocks):
    whole = jax.ShapeDtypeStruct((NZ, NX, NY), F32)
    anywhere = pl.BlockSpec(memory_space=pl.ANY)

    def vmem(*shape):
        return pltpu.VMEM(shape, F32)

    def dma(*shape):
        return pltpu.SemaphoreType.DMA(shape)

    full, plane = (NZ, NX, NY), (NX, NY)
    return pl.pallas_call(
        kernel,
        out_shape=(whole,) * 4,
        in_specs=[anywhere] * 8,
        out_specs=(anywhere,) * 4,
        scratch_shapes=[
            vmem(NZ, WIDE, NY), vmem(NZ, WIDE, NY),
            vmem(*full), vmem(*full), vmem(*full), vmem(NZ + 2, NX, NY),
            vmem(*full), vmem(*full), vmem(*full), vmem(*full), vmem(*full),
            vmem(*plane), vmem(*plane), vmem(*plane), vmem(*plane),
            vmem(2, *plane), vmem(2, *plane), vmem(*plane), vmem(*plane),
            vmem(4, NZ, NY),
            vmem(4, *plane), vmem(2, 4, NZ, NY),
            vmem(SUBSTEPS, 2, 2, *plane), vmem(SUBSTEPS, 2, 4, NZ, NY),
            vmem(2, *plane), vmem(2, 8, NY), vmem(2, *plane),
            vmem(3, *plane), vmem(LEVS, 3, *plane),
            vmem(4, *plane), vmem(SUBSTEPS, LEVS, 4, *plane), vmem(15, *plane),
            dma(8), dma(4),
            dma(4), dma(SUBSTEPS, 4), dma(3), dma(3), dma(3), dma(SUBSTEPS, 3),
            dma(4), dma(4), dma(2), dma(2),
        ],
        compiler_params=pltpu.CompilerParams(
            collective_id=0, has_side_effects=True, vmem_limit_bytes=40 * 1024 * 1024
        ),
        cost_estimate=pl.CostEstimate(flops=40_000_000, bytes_accessed=5_000_000, transcendentals=0),
    )(*blocks)


def solution(mesh):
    field, column = P("lev", "gx", "gy"), P("gx", "gy")
    return jax.shard_map(
        local,
        mesh=mesh,
        in_specs=(field, field, field, field, column, column, column, field),
        out_specs=(field, field, field, field),
        check_vma=False,
    )
```

```python
import jax
import jax.numpy as jnp
from jax import lax
from jax.experimental import pallas as pl
from jax.experimental.pallas import tpu as pltpu
from jax.sharding import PartitionSpec as P

SUBSTEPS = 2
GRAD = 0.35 / 12.0
VERT = 0.25

NZ, NX, NY = 32, 32, 128
GAP = 8
WIDE = NX + 2 * GAP
LEVS = 4
UNROLL = 8
F32 = jnp.float32
BF16 = jnp.bfloat16
CHUNK = 4


def level_rows(ref, row, first=0):
    levels, rows, lanes = ref.shape
    return ref.reshape(levels * rows, lanes), pl.ds(first * rows + row, NZ, stride=rows)


def get_rows(ref, row, first=0):
    flat, there = level_rows(ref, row, first)
    return flat[there, :]


def set_rows(ref, row, value, first=0):
    flat, there = level_rows(ref, row, first)
    flat[there, :] = value


def kernel(
    wx_h, wy_h, wz_h, p_h, plane_h, st_h,
    wx, wy, wz, pout,
    pbuf, fbuf, ps, st, inv, up_s, q_s, val,
    jac, ijac, slx, sly,
    wyp, npk, jpk, ijpk, nrow,
    ymsg, xmsg, yrecv, xrecv, jprecv, jrecv, strecv,
    vset, vsetrecv, vmsg, vrecv, coef,
    pt, qt, pd, qd, wpk, slypk, gsum, dpk, dmat,
    load_sem,
    hs_send, hs_recv, ss_send, ss_recv, vs_send, vs_recv, js_send, js_recv, es_send, es_recv,
):
    gx, gy, lev = lax.axis_index("gx"), lax.axis_index("gy"), lax.axis_index("lev")
    ngx, ngy = lax.axis_size("gx"), lax.axis_size("gy")
    xlo, xhi = lax.rem(gx + ngx - 1, ngx), lax.rem(gx + 1, ngx)
    ylo, yhi = lax.rem(gy + ngy - 1, ngy), lax.rem(gy + 1, ngy)
    up, down, over = lax.rem(lev + 1, LEVS), lax.rem(lev + 3, LEVS), lax.rem(lev + 2, LEVS)
    mesh_id = pl.DeviceIdType.MESH

    def remote(src, dst, send, recv, where):
        return pltpu.make_async_remote_copy(
            src_ref=src, dst_ref=dst, send_sem=send, recv_sem=recv,
            device_id=where, device_id_type=mesh_id,
        )

    loads = [
        pltpu.make_async_copy(src, dst, load_sem.at[i])
        for i, (src, dst) in enumerate((
            (p_h, pbuf.at[:, GAP:GAP + NX, :]), (wy_h, wy), (wx_h, wx), (plane_h.at[0], jac),
            (st_h, st), (plane_h.at[1], slx), (plane_h.at[2], sly), (wz_h, wz),
        ))
    ]
    for copy in loads:
        copy.start()
    barrier = pltpu.get_barrier_semaphore()
    partners = (
        {"gx": xlo}, {"gx": xhi}, {"gy": ylo}, {"gy": yhi},
        {"lev": up}, {"lev": down}, {"lev": over},
    )
    for where in partners:
        pl.semaphore_signal(barrier, inc=1, device_id=where, device_id_type=mesh_id)

    gap = jnp.zeros((GAP, NY), F32)

    def clear(l, carry):
        pbuf[l, 0:GAP, :] = gap
        pbuf[l, GAP + NX:WIDE, :] = gap
        fbuf[l, 0:GAP, :] = gap
        fbuf[l, GAP + NX:WIDE, :] = gap
        return carry

    lax.fori_loop(0, NZ, clear, 0, unroll=UNROLL)
    ps[0] = jnp.zeros((NX, NY), F32)
    ps[NZ + 1] = jnp.zeros((NX, NY), F32)

    lane = lax.broadcasted_iota(jnp.int32, (1, NY), 1)
    pos, group = lane & 7, lane >> 3

    def at(value, *places):
        hit = pos == places[0]
        for place in places[1:]:
            hit = hit | (pos == place)
        return jnp.where(hit, F32(value), F32(0))

    own_taps = (
        (2, at(1.0, 2, 3, 6, 7)), (1, at(-8.0, 1, 2, 3, 5, 6, 7)),
        (NY - 1, at(8.0, 0, 1, 2, 4, 5, 6)), (NY - 2, at(-1.0, 0, 1, 4, 5)),
    )
    far_taps = (
        (2, at(1.0, 4, 5)), (1, at(-8.0, 4)), (NY - 1, at(8.0, 3)), (NY - 2, at(-1.0, 2, 3)),
    )

    def taps(z, which):
        return sum(c * pltpu.roll(z, s, 1) for s, c in which)

    low_half, inner = pos < 4, (pos >= 2) & (pos <= 5)
    near_edge = (lane < 4) | (lane >= NY - 4)

    ahead = lax.broadcasted_iota(jnp.int32, (NY, NY), 0) - lax.broadcasted_iota(jnp.int32, (NY, NY), 1)
    band = jnp.zeros((NY, NY), F32)
    for k, c in ((-2, 1.0), (-1, -8.0), (1, 8.0), (2, -1.0)):
        band = jnp.where(ahead == k, F32(c), band)
    dmat[0:NY, :] = band.astype(BF16)
    dmat[NY:2 * NY, :] = band.astype(BF16)

    def lane_diff(f):
        flat = f.reshape(CHUNK * NX, NY)
        high = flat.astype(BF16)
        low = (flat - high.astype(F32)).astype(BF16)
        both = jnp.concatenate([high, low], axis=1)
        return jnp.dot(both, dmat[...], preferred_element_type=F32).reshape(CHUNK, NX, NY)

    acc0 = jnp.zeros((NX, NY), F32)
    def pack(sources):
        out = []
        for half in range(2):
            carry = [acc0] * len(sources)
            for i in range(16):
                here = group == i
                for k, src in enumerate(sources):
                    turned = pltpu.roll(src(half * 16 + i), (8 * i + 4) % NY, 1)
                    carry[k] = jnp.where(here, turned, carry[k])
            out.append(carry)
        return tuple(zip(*out))

    def spread_out(plane):
        z = jnp.where(lane < 8, pltpu.roll(plane, 4, 1), 0.0)
        for shift in (8, 16, 32, 64):
            z = z + pltpu.roll(z, shift, 1)
        return z

    def prow(r):
        return get_rows(pbuf, GAP + r)

    def jrow(r):
        return jac[r:r + 1, :]

    def y_copies(step):
        return (
            remote(ymsg.at[2:4], yrecv.at[step, 0], hs_send.at[0], hs_recv.at[step, 0], {"gy": yhi}),
            remote(ymsg.at[2:4], yrecv.at[step, 1], hs_send.at[1], hs_recv.at[step, 1], {"gy": ylo}),
        )

    def x_copies(step):
        return (
            remote(xmsg.at[1], xrecv.at[step, 0], hs_send.at[2], hs_recv.at[step, 2], {"gx": xhi}),
            remote(xmsg.at[0], xrecv.at[step, 1], hs_send.at[3], hs_recv.at[step, 3], {"gx": xlo}),
        )

    def edges_out(step):
        if step == 0:
            loads[0].wait()
            loads[2].wait()
            loads[3].wait()
        p0, p1, p2, p3 = (prow(r) for r in range(4))
        p28, p29, p30, p31 = (prow(r) for r in range(NX - 4, NX))
        n0 = get_rows(wx, 0) - GRAD * (8.0 * p1 - p2)
        n1 = get_rows(wx, 1) - GRAD * (8.0 * (p2 - p0) - p3)
        n30 = get_rows(wx, NX - 2) - GRAD * (p28 + 8.0 * (p31 - p29))
        n31 = get_rows(wx, NX - 1) - GRAD * (p29 - 8.0 * p30)
        for i, n in enumerate((n0, n1, n30, n31)):
            nrow[i] = n
        xmsg[0, 0] = p0
        xmsg[0, 1] = p1
        xmsg[0, 2] = jrow(0) * n0
        xmsg[0, 3] = jrow(1) * n1
        xmsg[1, 0] = p30
        xmsg[1, 1] = p31
        xmsg[1, 2] = jrow(NX - 2) * n30
        xmsg[1, 3] = jrow(NX - 1) * n31
        if step == 0:
            pl.semaphore_wait(barrier, len(partners))
        for copy in x_copies(step):
            copy.start()
        pressure = lambda l: pbuf[l, GAP:GAP + NX, :]
        if step == 0:
            jpk[...] = spread_out(jac[...])
            loads[1].wait()
            packed = pack((pressure, lambda l: wy[l]))
            for half in range(2):
                wyp[half] = packed[1][half]
        else:
            packed = pack((pressure,))
        for half in range(2):
            ymsg[half] = packed[0][half]
        jp = jpk[...]
        for half in range(2):
            pp = ymsg[half]
            n = wyp[half] - GRAD * taps(pp, own_taps)
            npk[half] = n
            flux = jp * n
            far = jnp.where(pos < 2, pltpu.roll(flux, NY - 2, 1), pltpu.roll(flux, 2, 1))
            ymsg[2 + half] = jnp.where(inner, pp, far)
        for copy in y_copies(step):
            copy.start()

    def edges_in(step):
        for copy in x_copies(step):
            copy.wait()
        p0, p1, p30, p31 = (xmsg[0, 0], xmsg[0, 1], xmsg[1, 0], xmsg[1, 1])
        low, high = xrecv.at[step, 0], xrecv.at[step, 1]
        jm2, jm1 = jrecv[0, 6:7, :], jrecv[0, 7:8, :]
        j32, j33 = jrecv[1, 0:1, :], jrecv[1, 1:2, :]
        pm2, pm1, p32, p33 = low[0], low[1], high[0], high[1]
        d0 = -GRAD * (pm2 - 8.0 * pm1)
        d1 = -GRAD * pm1
        d30 = GRAD * p32
        d31 = -GRAD * (8.0 * p32 - p33)
        fm2 = low[2] + (GRAD * jm2) * p0
        fm1 = low[3] - (GRAD * jm1) * (8.0 * p0 - p1)
        f32 = high[2] - (GRAD * j32) * (p30 - 8.0 * p31)
        f33 = high[3] - (GRAD * j33) * p31
        g0, g1 = jrow(0) * d0, jrow(1) * d1
        g30, g31 = jrow(NX - 2) * d30, jrow(NX - 1) * d31
        delta = {0: d0, 1: d1, NX - 2: d30, NX - 1: d31}
        for i, r in enumerate(delta):
            set_rows(wx, r, nrow[i] + delta[r])
        sums = (
            (0, fm2 + 8.0 * (g1 - fm1)), (1, fm1 - 8.0 * g0), (2, g0 - 8.0 * g1), (3, g1),
            (NX - 4, -g30), (NX - 3, 8.0 * g30 - g31), (NX - 2, 8.0 * g31 - f32),
            (NX - 1, 8.0 * (f32 - g30) - f33),
        )
        for r, s in sums:
            dp = (-GRAD * ijac[r:r + 1, :]) * s
            set_rows(ps, r, get_rows(ps, r, 1) + dp, 1)
            for side, (near, far) in enumerate(((pt, pd), (qt, qd))):
                change = get_rows(far, r) * dp
                if r in delta:
                    change = change + get_rows(near, r, 1) * (slx[r:r + 1, :] * delta[r])
                gsum[side, r:r + 1, :] = gsum[side, r:r + 1, :] + jnp.sum(change, axis=0, keepdims=True)

        for copy in y_copies(step):
            copy.wait()
        jp, ijp = jpk[...], ijpk[...]
        change = [acc0, acc0]
        jh = jnp.where(low_half, jprecv[0], jprecv[1])
        for half in range(2):
            m = jnp.where(low_half, yrecv[step, 0, half], yrecv[step, 1, half])
            pp = ymsg[half]
            d = -GRAD * taps(m, far_taps)
            part = jnp.where(low_half, pltpu.roll(m, 2, 1), pltpu.roll(m, NY - 2, 1))
            fh = part - GRAD * jh * taps(pp, far_taps)
            s = taps(jp * d, own_taps) + taps(fh, far_taps)
            wyp[half] = npk[half] + d
            dp = (-GRAD) * ijp * s
            dpk[0, half], dpk[1, half] = d, dp
            sd = slypk[...] * d
            change = [c + wpk[k, half] * sd + wpk[k + 2, half] * dp for k, c in enumerate(change)]
        for side in range(2):
            total = change[side]
            for shift in (8, 16, 32, 64):
                total = total + pltpu.roll(total, shift, 1)
            gsum[side] = gsum[side] + jnp.where(near_edge, pltpu.roll(total, 124, 1), 0.0)
        unpack_level(0, 0, 124)
        unpack_level(1, 15, 4)

    def unpack_level(half, i, shift):
        l = half * 16 + i
        wy[l] = wy[l] + jnp.where(near_edge, pltpu.roll(dpk[0, half], shift, 1), 0.0)
        ps[l + 1] = ps[l + 1] + jnp.where(near_edge, pltpu.roll(dpk[1, half], shift, 1), 0.0)

    def unpack_rest():
        for half in range(2):
            def unpack(i, carry):
                unpack_level(half, i, lax.rem(124 - 8 * i + NY, NY))
                return carry

            lax.fori_loop(1 - half, 16 - half, unpack, 0, unroll=5)

    def pre_source(l):
        return wz[l] + slx[...] * wx[l] + sly[...] * wy[l] - VERT * (ps[l + 2] - ps[l])

    def block_ends():
        def add(l, carry):
            rhs = pre_source(l)
            return carry[0] + pt[l + 1] * rhs, carry[1] + qt[l + 1] * rhs

        gsum[0], gsum[1] = lax.fori_loop(0, NZ, add, (acc0, acc0), unroll=UNROLL)

    def local_step():
        def row_diff(ref, lv):
            at_row = lambda k: ref[lv, GAP + k:GAP + NX + k, :]
            return (at_row(-2) - at_row(2)) + 8.0 * (at_row(1) - at_row(-1))

        def gradients(i, carry):
            lv = pl.ds(i * CHUNK, CHUNK)
            nx = wx[lv] - GRAD * row_diff(pbuf, lv)
            wx[lv] = nx
            fbuf[lv, GAP:GAP + NX, :] = jac[...] * nx
            wy[lv] = wy[lv] - GRAD * lane_diff(pbuf[lv, GAP:GAP + NX, :])
            return carry

        lax.fori_loop(0, NZ // CHUNK, gradients, 0, unroll=2)

        def divergence(i, carry):
            lv = pl.ds(i * CHUNK, CHUNK)
            spread = row_diff(fbuf, lv) + lane_diff(jac[...] * wy[lv])
            ps[pl.ds(i * CHUNK + 1, CHUNK)] = pbuf[lv, GAP:GAP + NX, :] - (GRAD * ijac[...]) * spread
            return carry

        lax.fori_loop(0, NZ // CHUNK, divergence, 0, unroll=2)

    jac_copies = (
        remote(jpk, jprecv.at[0], js_send.at[0], js_recv.at[0], {"gy": yhi}),
        remote(jpk, jprecv.at[1], js_send.at[1], js_recv.at[1], {"gy": ylo}),
        remote(jac.at[NX - 8:NX], jrecv.at[0], js_send.at[2], js_recv.at[2], {"gx": xhi}),
        remote(jac.at[0:8], jrecv.at[1], js_send.at[3], js_recv.at[3], {"gx": xlo}),
    )
    stiff_copies = (
        remote(st.at[NZ - 1], strecv.at[0], es_send.at[0], es_recv.at[0], {"lev": up}),
        remote(st.at[0], strecv.at[1], es_send.at[1], es_recv.at[1], {"lev": down}),
    )
    set_copies = (
        remote(vset, vsetrecv.at[lev], ss_send.at[0], ss_recv.at[0], {"lev": up}),
        remote(vset, vsetrecv.at[lev], ss_send.at[1], ss_recv.at[1], {"lev": down}),
        remote(vset, vsetrecv.at[lev], ss_send.at[2], ss_recv.at[2], {"lev": over}),
    )
    set_arrivals = (
        remote(vset, vsetrecv.at[down], ss_send.at[0], ss_recv.at[0], {"lev": up}),
        remote(vset, vsetrecv.at[up], ss_send.at[1], ss_recv.at[1], {"lev": down}),
        remote(vset, vsetrecv.at[over], ss_send.at[2], ss_recv.at[2], {"lev": over}),
    )

    def v_copies(step, arrivals):
        a, b, c = (down, up, over) if arrivals else (lev, lev, lev)
        return (
            remote(vmsg.at[1:4], vrecv.at[step, a, 1:4], vs_send.at[0], vs_recv.at[step, 0], {"lev": up}),
            remote(vmsg.at[0:3], vrecv.at[step, b, 0:3], vs_send.at[1], vs_recv.at[step, 1], {"lev": down}),
            remote(vmsg.at[1:3], vrecv.at[step, c, 1:3], vs_send.at[2], vs_recv.at[step, 2], {"lev": over}),
        )

    edges_out(0)
    for copy in jac_copies:
        copy.start()
    loads[4].wait()
    for copy in stiff_copies:
        copy.start()

    def factor(i, carry):
        rising, falling = carry
        h = NZ - 1 - i
        inv_l, inv_h = 1.0 / st[i], 1.0 / st[h]
        rising = 1.0 / (2.0 + inv_l - rising)
        falling = 1.0 / (2.0 + inv_h - falling)
        up_s[i] = rising
        val[h] = falling
        return rising, falling

    lax.fori_loop(0, NZ, factor, (acc0, acc0), unroll=UNROLL)

    def spikes(i, carry):
        below, above = carry
        h = NZ - 1 - i
        below = below * val[i]
        above = above * up_s[h]
        val[i] = below
        q_s[h] = above
        inv[i] = 1.0 / st[i]
        return below, above

    ones = jnp.ones((NX, NY), F32)
    lax.fori_loop(0, NZ, spikes, (ones, ones), unroll=UNROLL)
    p_s = st
    vset[0] = val[0]
    vset[1] = q_s[0]
    vset[2] = q_s[NZ - 1]
    for copy in set_copies:
        copy.start()
    for copy in stiff_copies:
        copy.wait()

    pt[0] = qt[0] = pt[NZ + 1] = qt[NZ + 1] = acc0

    def weigh(l, carry):
        p_s[l] = val[l]
        pt[l + 1] = val[l] * inv[l]
        qt[l + 1] = q_s[l] * inv[l]
        return carry

    lax.fori_loop(0, NZ, weigh, 0, unroll=UNROLL)

    def weigh_apart(l, carry):
        pd[l] = VERT * (pt[l + 2] - pt[l])
        qd[l] = VERT * (qt[l + 2] - qt[l])
        return carry

    lax.fori_loop(0, NZ, weigh_apart, 0, unroll=UNROLL)
    coef[13] = 1.0 / strecv[0]
    coef[14] = 1.0 / strecv[1]
    ijac[...] = 1.0 / jac[...]
    ijpk[...] = 1.0 / jpk[...]
    for copy in loads[5:]:
        copy.wait()
    slypk[...] = spread_out(sly[...])

    def after_setup():
        for copy in set_copies:
            copy.wait_send()
        for copy in set_arrivals:
            copy.wait_recv()
        vsetrecv[lev] = vset[...]
        pa = [vsetrecv[i, 0] for i in range(LEVS)]
        qa = [vsetrecv[i, 1] for i in range(LEVS)]
        qb = [vsetrecv[i, 2] for i in range(LEVS)]
        b0 = qb[0]
        t1 = qa[1] / (1.0 - b0 * pa[1])
        b1 = qb[1] + t1 * b0 * qa[1]
        t2 = qa[2] / (1.0 - b1 * pa[2])
        b2 = qb[2] + t2 * b1 * qa[2]
        e3 = pa[3]
        r2 = qa[2] / (1.0 - e3 * qb[2])
        e2 = pa[2] + r2 * e3 * qa[2]
        r1 = qa[1] / (1.0 - e2 * qb[1])
        e1 = pa[1] + r1 * e2 * qa[1]
        z0 = 1.0 / (1.0 - b0 * e1)
        z1 = 1.0 / (1.0 - b1 * e2)
        z2 = 1.0 / (1.0 - b2 * e3)
        for i, c in enumerate((t1, b0, b1, t2, r1, r2, e2, e3, e1, b2, z0, z1, z2)):
            coef[i] = c

    def pick(*values):
        out = values[-1]
        for i in range(LEVS - 2, -1, -1):
            out = jnp.where(lev == i, values[i], out)
        return out

    for step in range(SUBSTEPS):
        last = step == SUBSTEPS - 1
        if step > 0:
            edges_out(step)
        local_step()
        block_ends()
        if step == 0:
            packed = pack((lambda l: pt[l + 1], lambda l: qt[l + 1], lambda l: pd[l], lambda l: qd[l]))
            for k in range(4):
                for half in range(2):
                    wpk[k, half] = packed[k][half]
            for copy in jac_copies:
                copy.wait()
        edges_in(step)
        vmsg[0] = ps[1]
        vmsg[1] = gsum[0] - VERT * ps[1] * coef[13]
        vmsg[2] = gsum[1] + VERT * ps[NZ] * coef[14]
        vmsg[3] = ps[NZ]
        for copy in v_copies(step, False):
            copy.start()
        unpack_rest()

        def rising(l, v):
            v = (pre_source(l) * inv[l] + v) * up_s[l]
            val[l] = v
            return v

        top = lax.fori_loop(0, NZ, rising, acc0, unroll=UNROLL)

        def falling(i, x):
            l = NZ - 2 - i
            x = val[l] + up_s[l] * x
            val[l] = x
            return x

        lax.fori_loop(0, NZ - 1, falling, top, unroll=UNROLL)
        if step == 0:
            after_setup()

        for copy in v_copies(step, False):
            copy.wait_send()
        for copy in v_copies(step, True):
            copy.wait_recv()
        vrecv[step, lev] = vmsg[...]
        ga = [vrecv[step, i, 1] for i in range(LEVS)]
        gb = [vrecv[step, i, 2] for i in range(LEVS)]
        t1, b0, b1, t2, r1, r2, e2, e3, e1, b2, z0, z1, z2 = (coef[i] for i in range(13))
        a0 = gb[0]
        a1 = gb[1] + t1 * (a0 + b0 * ga[1])
        a2 = gb[2] + t2 * (a1 + b1 * ga[2])
        c3 = ga[3]
        c2 = ga[2] + r2 * (c3 + e3 * gb[2])
        c1 = ga[1] + r1 * (c2 + e2 * gb[1])
        w = pick(acc0, (a0 + b0 * c1) * z0, (a1 + b1 * c2) * z1, (a2 + b2 * c3) * z2)
        y = pick((c1 + e1 * a0) * z0, (c2 + e2 * a1) * z1, (c3 + e3 * a2) * z2, acc0)
        under = jnp.where(lev == 0, acc0, w - VERT * vrecv[step, down, 3] * inv[0])
        above = jnp.where(lev == LEVS - 1, acc0, y + VERT * vrecv[step, up, 0] * inv[NZ - 1])

        def solved(l):
            return val[l] + p_s[l] * w + q_s[l] * y

        def keep_pressure(l, p):
            if last:
                pout[l] = p
            else:
                pbuf[l, GAP:GAP + NX, :] = p

        def finish(l, carry):
            before, here = carry
            after = solved(l + 1)
            wz[l] = here
            keep_pressure(l, ps[l + 1] - VERT * (after - before))
            return here, after

        before, here = lax.fori_loop(0, NZ - 1, finish, (under, solved(0)), unroll=UNROLL)
        wz[NZ - 1] = here
        keep_pressure(NZ - 1, ps[NZ] - VERT * (above - before))


def store(*refs):
    sems = refs[-1]
    copies = [pltpu.make_async_copy(refs[i], refs[4 + i], sems.at[i]) for i in range(4)]
    for copy in copies:
        copy.start()
    for copy in copies:
        copy.wait()


def local(*blocks):
    whole = jax.ShapeDtypeStruct((NZ, NX, NY), F32)
    anywhere, hbm = pl.BlockSpec(memory_space=pl.ANY), pl.BlockSpec(memory_space=pltpu.HBM)

    def vmem(*shape):
        return pltpu.VMEM(shape, F32)

    def dma(*shape):
        return pltpu.SemaphoreType.DMA(shape)

    full, plane = (NZ, NX, NY), (NX, NY)
    blocks = pl.pallas_call(
        kernel,
        out_shape=(whole,) * 4,
        in_specs=[hbm] * 6,
        out_specs=(pl.BlockSpec(memory_space=pltpu.VMEM),) * 4,
        scratch_shapes=[
            vmem(NZ, WIDE, NY), vmem(NZ, WIDE, NY),
            vmem(NZ + 2, NX, NY),
            vmem(*full), vmem(*full), vmem(*full), vmem(*full), vmem(*full),
            vmem(*plane), vmem(*plane), vmem(*plane), vmem(*plane),
            vmem(2, *plane), vmem(2, *plane), vmem(*plane), vmem(*plane),
            vmem(4, NZ, NY),
            vmem(4, *plane), vmem(2, 4, NZ, NY),
            vmem(SUBSTEPS, 2, 2, *plane), vmem(SUBSTEPS, 2, 4, NZ, NY),
            vmem(2, *plane), vmem(2, 8, NY), vmem(2, *plane),
            vmem(3, *plane), vmem(LEVS, 3, *plane),
            vmem(4, *plane), vmem(SUBSTEPS, LEVS, 4, *plane), vmem(15, *plane),
            vmem(NZ + 2, NX, NY), vmem(NZ + 2, NX, NY), vmem(*full), vmem(*full),
            vmem(4, 2, *plane), vmem(*plane), vmem(2, *plane), vmem(2, 2, *plane),
            pltpu.VMEM((2 * NY, NY), BF16),
            dma(8),
            dma(4), dma(SUBSTEPS, 4), dma(3), dma(3), dma(3), dma(SUBSTEPS, 3),
            dma(4), dma(4), dma(2), dma(2),
        ],
        compiler_params=pltpu.CompilerParams(
            collective_id=0, has_side_effects=True, vmem_limit_bytes=53000 * 1024
        ),
    )(*blocks[:4], jnp.stack(blocks[4:7]), blocks[7])
    return pl.pallas_call(
        store,
        out_shape=(whole,) * 4,
        in_specs=[anywhere] * 4,
        out_specs=(hbm,) * 4,
        scratch_shapes=[dma(4)],
        compiler_params=pltpu.CompilerParams(vmem_limit_bytes=1024 * 1024),
        cost_estimate=pl.CostEstimate(flops=0, bytes_accessed=4_000_000, transcendentals=0),
    )(*blocks)


def solution(mesh):
    field, column = P("lev", "gx", "gy"), P("gx", "gy")
    return jax.shard_map(
        local,
        mesh=mesh,
        in_specs=(field, field, field, field, column, column, column, field),
        out_specs=(field, field, field, field),
        check_vma=False,
    )
```

```python
import jax
import jax.numpy as jnp
from jax import lax
from jax.experimental import pallas as pl
from jax.experimental.pallas import tpu as pltpu
from jax.sharding import PartitionSpec as P

SUBSTEPS = 2
GRAD = 0.35 / 12.0
VERT = 0.25

NZ, NX, NY = 32, 32, 128
GAP = 8
WIDE = NX + 2 * GAP
LEVS = 4
UNROLL = 8
F32 = jnp.float32
BF16 = jnp.bfloat16
CHUNK = 4
EDGE_ROWS = (0, 1, 2, 3, NX - 4, NX - 3, NX - 2, NX - 1)
FLUX_ROWS = (0, 1, NX - 2, NX - 1)


def level_rows(ref, row, first=0):
    levels, rows, lanes = ref.shape
    return ref.reshape(levels * rows, lanes), pl.ds(first * rows + row, NZ, stride=rows)


def get_rows(ref, row, first=0):
    flat, there = level_rows(ref, row, first)
    return flat[there, :]


def set_rows(ref, row, value, first=0):
    flat, there = level_rows(ref, row, first)
    flat[there, :] = value


def kernel(
    wx_h, wy_h, wz_h, p_h, plane_h, st_h,
    wx, wy, wz, pout,
    pbuf, fbuf, ps, st, inv, up_s, q_s, val,
    jac, ijac, slx, sly,
    wyp, npk, jpk, ijpk, nrow,
    ymsg, xmsg, yrecv, xrecv, jprecv, jrecv, strecv,
    vset, vsetrecv, vmsg, vrecv, coef,
    pt, qt, pd, qd, wpk, slypk, gsum, dpk, dmat, p_s, xw, dpx, farp,
    load_sem,
    hs_send, hs_recv, ss_send, ss_recv, vs_send, vs_recv, js_send, js_recv, es_send, es_recv,
):
    gx, gy, lev = lax.axis_index("gx"), lax.axis_index("gy"), lax.axis_index("lev")
    ngx, ngy = lax.axis_size("gx"), lax.axis_size("gy")
    xlo, xhi = lax.rem(gx + ngx - 1, ngx), lax.rem(gx + 1, ngx)
    ylo, yhi = lax.rem(gy + ngy - 1, ngy), lax.rem(gy + 1, ngy)
    up, down, over = lax.rem(lev + 1, LEVS), lax.rem(lev + 3, LEVS), lax.rem(lev + 2, LEVS)
    mesh_id = pl.DeviceIdType.MESH

    def remote(src, dst, send, recv, where):
        return pltpu.make_async_remote_copy(
            src_ref=src, dst_ref=dst, send_sem=send, recv_sem=recv,
            device_id=where, device_id_type=mesh_id,
        )

    loads = [
        pltpu.make_async_copy(src, dst, load_sem.at[i])
        for i, (src, dst) in enumerate((
            (p_h, pbuf.at[:, GAP:GAP + NX, :]), (wy_h, wy), (wx_h, wx), (plane_h.at[0], jac),
            (st_h, st), (plane_h.at[1], slx), (plane_h.at[2], sly), (wz_h, wz),
        ))
    ]
    for copy in loads:
        copy.start()
    barrier = pltpu.get_barrier_semaphore()
    partners = (
        {"gx": xlo}, {"gx": xhi}, {"gy": ylo}, {"gy": yhi},
        {"lev": up}, {"lev": down}, {"lev": over},
    )
    for where in partners:
        pl.semaphore_signal(barrier, inc=1, device_id=where, device_id_type=mesh_id)

    gap = jnp.zeros((GAP, NY), F32)

    def clear(l, carry):
        pbuf[l, 0:GAP, :] = gap
        pbuf[l, GAP + NX:WIDE, :] = gap
        fbuf[l, 0:GAP, :] = gap
        fbuf[l, GAP + NX:WIDE, :] = gap
        return carry

    lax.fori_loop(0, NZ, clear, 0, unroll=UNROLL)
    ps[0] = jnp.zeros((NX, NY), F32)
    ps[NZ + 1] = jnp.zeros((NX, NY), F32)

    lane = lax.broadcasted_iota(jnp.int32, (1, NY), 1)
    pos, group = lane & 7, lane >> 3

    def at(value, *places):
        hit = pos == places[0]
        for place in places[1:]:
            hit = hit | (pos == place)
        return jnp.where(hit, F32(value), F32(0))

    own_taps = (
        (2, at(1.0, 2, 3, 6, 7)), (1, at(-8.0, 1, 2, 3, 5, 6, 7)),
        (NY - 1, at(8.0, 0, 1, 2, 4, 5, 6)), (NY - 2, at(-1.0, 0, 1, 4, 5)),
    )
    far_taps = (
        (2, at(1.0, 4, 5)), (1, at(-8.0, 4)), (NY - 1, at(8.0, 3)), (NY - 2, at(-1.0, 2, 3)),
    )

    flux_taps = (
        (2, at(1.0, 4, 5), at(1.0, 2, 3)), (1, at(-8.0, 2, 4, 5), at(-8.0, 3)),
        (NY - 1, at(8.0, 2, 3, 5), at(8.0, 4)), (NY - 2, at(-1.0, 2, 3), at(-1.0, 4, 5)),
    )

    def taps(z, which):
        return sum(c * pltpu.roll(z, s, 1) for s, c in which)

    low_half, inner = pos < 4, (pos >= 2) & (pos <= 5)
    near_edge = (lane < 4) | (lane >= NY - 4)

    ahead = lax.broadcasted_iota(jnp.int32, (NY, NY), 0) - lax.broadcasted_iota(jnp.int32, (NY, NY), 1)
    band = jnp.zeros((NY, NY), F32)
    for k, c in ((-2, 1.0), (-1, -8.0), (1, 8.0), (2, -1.0)):
        band = jnp.where(ahead == k, F32(c), band)
    dmat[0:NY, :] = band.astype(BF16)
    dmat[NY:2 * NY, :] = band.astype(BF16)

    def lane_diff(f):
        flat = f.reshape(CHUNK * NX, NY)
        high = flat.astype(BF16)
        low = (flat - high.astype(F32)).astype(BF16)
        both = jnp.concatenate([high, low], axis=1)
        return jnp.dot(both, dmat[...], preferred_element_type=F32).reshape(CHUNK, NX, NY)

    acc0 = jnp.zeros((NX, NY), F32)
    def pack(sources):
        out = []
        for half in range(2):
            carry = [acc0] * len(sources)
            for i in range(16):
                here = group == i
                for k, src in enumerate(sources):
                    turned = pltpu.roll(src(half * 16 + i), (8 * i + 4) % NY, 1)
                    carry[k] = jnp.where(here, turned, carry[k])
            out.append(carry)
        return tuple(zip(*out))

    def spread_out(plane):
        z = jnp.where(lane < 8, pltpu.roll(plane, 4, 1), 0.0)
        for shift in (8, 16, 32, 64):
            z = z + pltpu.roll(z, shift, 1)
        return z

    def prow(r):
        return get_rows(pbuf, GAP + r)

    def jrow(r):
        return jac[r:r + 1, :]

    def y_copies(step):
        return (
            remote(ymsg.at[2:4], yrecv.at[step, 0], hs_send.at[0], hs_recv.at[step, 0], {"gy": yhi}),
            remote(ymsg.at[2:4], yrecv.at[step, 1], hs_send.at[1], hs_recv.at[step, 1], {"gy": ylo}),
        )

    def x_copies(step):
        return (
            remote(xmsg.at[1], xrecv.at[step, 0], hs_send.at[2], hs_recv.at[step, 2], {"gx": xhi}),
            remote(xmsg.at[0], xrecv.at[step, 1], hs_send.at[3], hs_recv.at[step, 3], {"gx": xlo}),
        )

    def edges_out(step):
        if step == 0:
            loads[0].wait()
            loads[2].wait()
            loads[3].wait()
        p0, p1, p2, p3 = (prow(r) for r in range(4))
        p28, p29, p30, p31 = (prow(r) for r in range(NX - 4, NX))
        wind_row = lambda i: nrow[i] if step else get_rows(wx, FLUX_ROWS[i])
        n0 = wind_row(0) - GRAD * (8.0 * p1 - p2)
        n1 = wind_row(1) - GRAD * (8.0 * (p2 - p0) - p3)
        n30 = wind_row(2) - GRAD * (p28 + 8.0 * (p31 - p29))
        n31 = wind_row(3) - GRAD * (p29 - 8.0 * p30)
        for i, n in enumerate((n0, n1, n30, n31)):
            nrow[i] = n
        xmsg[0, 0] = p0
        xmsg[0, 1] = p1
        xmsg[0, 2] = jrow(0) * n0
        xmsg[0, 3] = jrow(1) * n1
        xmsg[1, 0] = p30
        xmsg[1, 1] = p31
        xmsg[1, 2] = jrow(NX - 2) * n30
        xmsg[1, 3] = jrow(NX - 1) * n31
        if step == 0:
            pl.semaphore_wait(barrier, len(partners))
        for copy in x_copies(step):
            copy.start()
        if step == 0:
            columns()
        pressure = lambda l: pbuf[l, GAP:GAP + NX, :]
        if step == 0:
            jpk[...] = spread_out(jac[...])
            loads[1].wait()
            packed = pack((pressure, lambda l: wy[l]))
            for half in range(2):
                wyp[half] = packed[1][half]
        else:
            packed = pack((pressure,))
        for half in range(2):
            ymsg[half] = packed[0][half]
        jp = jpk[...]
        for half in range(2):
            pp = ymsg[half]
            n = wyp[half] - GRAD * taps(pp, own_taps)
            npk[half] = n
            flux = jp * n
            far = jnp.where(pos < 2, pltpu.roll(flux, NY - 2, 1), pltpu.roll(flux, 2, 1))
            ymsg[2 + half] = jnp.where(inner, pp, far)
        for copy in y_copies(step):
            copy.start()
        far_parts()

    def far_parts():
        for half in range(2):
            farp[half] = taps(ymsg[half], far_taps)

    def edges_in(step):
        for copy in x_copies(step):
            copy.wait()
        p0, p1, p30, p31 = (xmsg[0, 0], xmsg[0, 1], xmsg[1, 0], xmsg[1, 1])
        low, high = xrecv.at[step, 0], xrecv.at[step, 1]
        jm2, jm1 = jrecv[0, 6:7, :], jrecv[0, 7:8, :]
        j32, j33 = jrecv[1, 0:1, :], jrecv[1, 1:2, :]
        pm2, pm1, p32, p33 = low[0], low[1], high[0], high[1]
        d0 = -GRAD * (pm2 - 8.0 * pm1)
        d1 = -GRAD * pm1
        d30 = GRAD * p32
        d31 = -GRAD * (8.0 * p32 - p33)
        fm2 = low[2] + (GRAD * jm2) * p0
        fm1 = low[3] - (GRAD * jm1) * (8.0 * p0 - p1)
        f32 = high[2] - (GRAD * j32) * (p30 - 8.0 * p31)
        f33 = high[3] - (GRAD * j33) * p31
        g0, g1 = jrow(0) * d0, jrow(1) * d1
        g30, g31 = jrow(NX - 2) * d30, jrow(NX - 1) * d31
        delta = {0: d0, 1: d1, NX - 2: d30, NX - 1: d31}
        for i, r in enumerate(FLUX_ROWS):
            nrow[i] = nrow[i] + delta[r]
        sums = (
            fm2 + 8.0 * (g1 - fm1), fm1 - 8.0 * g0, g0 - 8.0 * g1, g1,
            -g30, 8.0 * g30 - g31, 8.0 * g31 - f32, 8.0 * (f32 - g30) - f33,
        )
        for i, (r, s) in enumerate(zip(EDGE_ROWS, sums)):
            dp = (-GRAD * ijac[r:r + 1, :]) * s
            dpx[i] = dp
            ps[1, r:r + 1, :] = ps[1, r:r + 1, :] + dp[0:1, :]
            ps[NZ, r:r + 1, :] = ps[NZ, r:r + 1, :] + dp[NZ - 1:NZ, :]
            for side in range(2):
                change = xw[side, i] * dp
                if r in delta:
                    change = change + xw[side, 8 + FLUX_ROWS.index(r)] * delta[r]
                gsum[side, r:r + 1, :] = gsum[side, r:r + 1, :] + jnp.sum(change, axis=0, keepdims=True)

        for copy in y_copies(step):
            copy.wait()
        jp, ijp = jpk[...], ijpk[...]
        change = [acc0, acc0]
        jh = jnp.where(low_half, jprecv[0], jprecv[1])
        for half in range(2):
            m = jnp.where(low_half, yrecv[step, 0, half], yrecv[step, 1, half])
            turned = [pltpu.roll(m, k, 1) for k, _ in far_taps]
            d = -GRAD * sum(c * t for (_, c), t in zip(far_taps, turned))
            fh = jnp.where(low_half, turned[0], turned[3]) - GRAD * jh * farp[half]
            g = jp * d
            s = sum(
                pltpu.roll(jnp.where(inner, own * g + far * fh, 0.0), k, 1)
                for k, own, far in flux_taps
            )
            wyp[half] = npk[half] + d
            dp = (-GRAD) * ijp * s
            dpk[0, half], dpk[1, half] = d, dp
            sd = slypk[...] * d
            change = [c + wpk[k, half] * sd + wpk[k + 2, half] * dp for k, c in enumerate(change)]
        for side in range(2):
            total = change[side]
            for shift in (8, 16, 32, 64):
                total = total + pltpu.roll(total, shift, 1)
            gsum[side] = gsum[side] + jnp.where(near_edge, pltpu.roll(total, 124, 1), 0.0)
        unpack_level(0, 0, 124)
        unpack_level(1, 15, 4)

    def unpack_level(half, i, shift):
        l = half * 16 + i
        wy[l] = wy[l] + jnp.where(near_edge, pltpu.roll(dpk[0, half], shift, 1), 0.0)
        ps[l + 1] = ps[l + 1] + jnp.where(near_edge, pltpu.roll(dpk[1, half], shift, 1), 0.0)

    def unpack_rest():
        for half in range(2):
            def unpack(i, carry):
                unpack_level(half, i, lax.rem(124 - 8 * i + NY, NY))
                return carry

            lax.fori_loop(1 - half, 16 - half, unpack, 0, unroll=5)

    def pre_source(l):
        return wz[l] + slx[...] * wx[l] + sly[...] * wy[l] - VERT * (ps[l + 2] - ps[l])

    def block_ends():
        def add(l, carry):
            rhs = pre_source(l)
            return carry[0] + pt[l + 1] * rhs, carry[1] + qt[l + 1] * rhs

        gsum[0], gsum[1] = lax.fori_loop(0, NZ, add, (acc0, acc0), unroll=UNROLL)

    def local_step():
        def row_diff(ref, lv):
            at_row = lambda k: ref[lv, GAP + k:GAP + NX + k, :]
            return (at_row(-2) - at_row(2)) + 8.0 * (at_row(1) - at_row(-1))

        def gradients(i, carry):
            lv = pl.ds(i * CHUNK, CHUNK)
            nx = wx[lv] - GRAD * row_diff(pbuf, lv)
            wx[lv] = nx
            fbuf[lv, GAP:GAP + NX, :] = jac[...] * nx
            wy[lv] = wy[lv] - GRAD * lane_diff(pbuf[lv, GAP:GAP + NX, :])
            return carry

        lax.fori_loop(0, NZ // CHUNK, gradients, 0, unroll=2)

        def divergence(i, carry):
            lv = pl.ds(i * CHUNK, CHUNK)
            spread = row_diff(fbuf, lv) + lane_diff(jac[...] * wy[lv])
            ps[pl.ds(i * CHUNK + 1, CHUNK)] = pbuf[lv, GAP:GAP + NX, :] - (GRAD * ijac[...]) * spread
            return carry

        lax.fori_loop(0, NZ // CHUNK, divergence, 0, unroll=2)

    jac_copies = (
        remote(jpk, jprecv.at[0], js_send.at[0], js_recv.at[0], {"gy": yhi}),
        remote(jpk, jprecv.at[1], js_send.at[1], js_recv.at[1], {"gy": ylo}),
        remote(jac.at[NX - 8:NX], jrecv.at[0], js_send.at[2], js_recv.at[2], {"gx": xhi}),
        remote(jac.at[0:8], jrecv.at[1], js_send.at[3], js_recv.at[3], {"gx": xlo}),
    )
    stiff_copies = (
        remote(st.at[NZ - 1], strecv.at[0], es_send.at[0], es_recv.at[0], {"lev": up}),
        remote(st.at[0], strecv.at[1], es_send.at[1], es_recv.at[1], {"lev": down}),
    )
    set_copies = (
        remote(vset, vsetrecv.at[lev], ss_send.at[0], ss_recv.at[0], {"lev": up}),
        remote(vset, vsetrecv.at[lev], ss_send.at[1], ss_recv.at[1], {"lev": down}),
        remote(vset, vsetrecv.at[lev], ss_send.at[2], ss_recv.at[2], {"lev": over}),
    )
    set_arrivals = (
        remote(vset, vsetrecv.at[down], ss_send.at[0], ss_recv.at[0], {"lev": up}),
        remote(vset, vsetrecv.at[up], ss_send.at[1], ss_recv.at[1], {"lev": down}),
        remote(vset, vsetrecv.at[over], ss_send.at[2], ss_recv.at[2], {"lev": over}),
    )

    def v_copies(step):
        return (
            remote(vmsg.at[3:5], vrecv.at[step, 0], vs_send.at[0], vs_recv.at[step, 0], {"lev": up}),
            remote(vmsg.at[0:2], vrecv.at[step, 1], vs_send.at[1], vs_recv.at[step, 1], {"lev": down}),
            remote(vmsg.at[2:3], vrecv.at[step, 2, 0:1], vs_send.at[2], vs_recv.at[step, 2], {"lev": over}),
        )

    def columns():
        loads[4].wait()
        for copy in stiff_copies:
            copy.start()

        def factor(i, carry):
            rising, falling = carry
            h = NZ - 1 - i
            inv_l, inv_h = 1.0 / st[i], 1.0 / st[h]
            rising = 1.0 / (2.0 + inv_l - rising)
            falling = 1.0 / (2.0 + inv_h - falling)
            up_s[i] = rising
            val[h] = falling
            return rising, falling

        lax.fori_loop(0, NZ, factor, (acc0, acc0), unroll=UNROLL)

        def spikes(i, carry):
            below, above = carry
            h = NZ - 1 - i
            below = below * val[i]
            above = above * up_s[h]
            p_s[i] = below
            q_s[h] = above
            inv[i] = 1.0 / st[i]
            return below, above

        ones = jnp.ones((NX, NY), F32)
        lax.fori_loop(0, NZ, spikes, (ones, ones), unroll=UNROLL)
        vset[0] = p_s[0]
        vset[1] = q_s[0]
        vset[2] = q_s[NZ - 1]
        for copy in set_copies:
            copy.start()

    edges_out(0)
    for copy in jac_copies:
        copy.start()

    pt[0] = qt[0] = pt[NZ + 1] = qt[NZ + 1] = acc0

    def weigh(l, carry):
        pt[l + 1] = p_s[l] * inv[l]
        qt[l + 1] = q_s[l] * inv[l]
        return carry

    lax.fori_loop(0, NZ, weigh, 0, unroll=UNROLL)

    def weigh_apart(l, carry):
        pd[l] = VERT * (pt[l + 2] - pt[l])
        qd[l] = VERT * (qt[l + 2] - qt[l])
        return carry

    lax.fori_loop(0, NZ, weigh_apart, 0, unroll=UNROLL)
    ijac[...] = 1.0 / jac[...]
    ijpk[...] = 1.0 / jpk[...]
    for copy in loads[5:]:
        copy.wait()
    slypk[...] = spread_out(sly[...])

    depth = lax.broadcasted_iota(jnp.int32, (NZ, NY), 0)
    inside = (depth > 0) & (depth < NZ - 1)

    def pick(*values):
        out = values[-1]
        for i in range(LEVS - 2, -1, -1):
            out = jnp.where(lev == i, values[i], out)
        return out

    def after_setup():
        for copy in set_copies:
            copy.wait_send()
        for copy in set_arrivals:
            copy.wait_recv()
        vsetrecv[lev] = vset[...]
        pa = [vsetrecv[i, 0] for i in range(LEVS)]
        qa = [vsetrecv[i, 1] for i in range(LEVS)]
        qb = [vsetrecv[i, 2] for i in range(LEVS)]
        b0 = qb[0]
        t1 = qa[1] / (1.0 - b0 * pa[1])
        b1 = qb[1] + t1 * b0 * qa[1]
        t2 = qa[2] / (1.0 - b1 * pa[2])
        b2 = qb[2] + t2 * b1 * qa[2]
        e3 = pa[3]
        r2 = qa[2] / (1.0 - e3 * qb[2])
        e2 = pa[2] + r2 * e3 * qa[2]
        r1 = qa[1] / (1.0 - e2 * qb[1])
        e1 = pa[1] + r1 * e2 * qa[1]
        z0 = 1.0 / (1.0 - b0 * e1)
        z1 = 1.0 / (1.0 - b1 * e2)
        z2 = 1.0 / (1.0 - b2 * e3)
        for i, c in enumerate((t1, b0, b1, t2, r1, r2, e2, e3, e1, b2, z0, z1, z2)):
            coef[i] = c
        coef[15] = pick(acc0, t1 * b0, t2 * b1, acc0)
        coef[16] = pick(acc0, r1 * e2, r2 * e3, acc0)

    for step in range(SUBSTEPS):
        last = step == SUBSTEPS - 1
        if step > 0:
            edges_out(step)
        local_step()
        block_ends()
        if step == 0:
            packed = pack((lambda l: pt[l + 1], lambda l: qt[l + 1], lambda l: pd[l], lambda l: qd[l]))
            for k in range(4):
                for half in range(2):
                    wpk[k, half] = packed[k][half]
            for side, (near, far) in enumerate(((pt, pd), (qt, qd))):
                for i, r in enumerate(EDGE_ROWS):
                    xw[side, i] = get_rows(far, r)
                for i, r in enumerate(FLUX_ROWS):
                    xw[side, 8 + i] = slx[r:r + 1, :] * get_rows(near, r, 1)
            for copy in jac_copies + stiff_copies:
                copy.wait()
            coef[13] = 1.0 / strecv[0]
            coef[14] = 1.0 / strecv[1]
            after_setup()
        edges_in(step)
        ga = gsum[0] - VERT * ps[1] * coef[13]
        gb = gsum[1] + VERT * ps[NZ] * coef[14]
        own_mu = gb + coef[15] * ga
        own_nu = ga + coef[16] * gb
        vmsg[0] = ps[1]
        vmsg[1] = jnp.where(lev == 0, own_mu, own_nu)
        vmsg[2] = jnp.where(lev < 2, own_mu, own_nu)
        vmsg[3] = jnp.where(lev == LEVS - 1, own_nu, own_mu)
        vmsg[4] = ps[NZ]
        for copy in v_copies(step):
            copy.start()
        gsum[0], gsum[1] = own_mu, own_nu
        for i, r in enumerate(FLUX_ROWS):
            set_rows(wx, r, nrow[i])
        for i, r in enumerate(EDGE_ROWS):
            there = dpx[i]
            set_rows(ps, r, get_rows(ps, r, 1) + jnp.where(inside, there, 0.0), 1)
        unpack_rest()

        def rising(l, v):
            v = (pre_source(l) * inv[l] + v) * up_s[l]
            val[l] = v
            return v

        top = lax.fori_loop(0, NZ, rising, acc0, unroll=UNROLL)

        def falling(i, x):
            l = NZ - 2 - i
            x = val[l] + up_s[l] * x
            val[l] = x
            return x

        lax.fori_loop(0, NZ - 1, falling, top, unroll=UNROLL)
        for copy in v_copies(step):
            copy.wait()
        own_mu, own_nu = gsum[0], gsum[1]
        low, high, far = vrecv[step, 0, 0], vrecv[step, 1, 1], vrecv[step, 2, 0]
        t1, b0, b1, t2, r1, r2, e2, e3, e1, b2, z0, z1, z2 = (coef[i] for i in range(13))
        a0 = pick(own_mu, low, far, high)
        a1 = pick(acc0, own_mu, low, far) + t1 * a0
        a2 = pick(acc0, acc0, own_mu, low) + t2 * a1
        c3 = pick(low, far, high, own_nu)
        c2 = pick(far, high, own_nu, acc0) + r2 * c3
        c1 = pick(high, own_nu, acc0, acc0) + r1 * c2
        w = pick(acc0, (a0 + b0 * c1) * z0, (a1 + b1 * c2) * z1, (a2 + b2 * c3) * z2)
        y = pick((c1 + e1 * a0) * z0, (c2 + e2 * a1) * z1, (c3 + e3 * a2) * z2, acc0)
        under = jnp.where(lev == 0, acc0, w - VERT * vrecv[step, 0, 1] * inv[0])
        above = jnp.where(lev == LEVS - 1, acc0, y + VERT * vrecv[step, 1, 0] * inv[NZ - 1])

        def solved(l):
            return val[l] + p_s[l] * w + q_s[l] * y

        def keep_pressure(l, p):
            if last:
                pout[l] = p
            else:
                pbuf[l, GAP:GAP + NX, :] = p

        def finish(l, carry):
            before, here = carry
            after = solved(l + 1)
            wz[l] = here
            keep_pressure(l, ps[l + 1] - VERT * (after - before))
            return here, after

        before, here = lax.fori_loop(0, NZ - 1, finish, (under, solved(0)), unroll=UNROLL)
        wz[NZ - 1] = here
        keep_pressure(NZ - 1, ps[NZ] - VERT * (above - before))


def store(*refs):
    sems = refs[-1]
    copies = [pltpu.make_async_copy(refs[i], refs[4 + i], sems.at[i]) for i in range(4)]
    for copy in copies:
        copy.start()
    for copy in copies:
        copy.wait()


def local(*blocks):
    whole = jax.ShapeDtypeStruct((NZ, NX, NY), F32)
    anywhere, hbm = pl.BlockSpec(memory_space=pl.ANY), pl.BlockSpec(memory_space=pltpu.HBM)

    def vmem(*shape):
        return pltpu.VMEM(shape, F32)

    def dma(*shape):
        return pltpu.SemaphoreType.DMA(shape)

    full, plane = (NZ, NX, NY), (NX, NY)
    blocks = pl.pallas_call(
        kernel,
        out_shape=(whole,) * 4,
        in_specs=[hbm] * 6,
        out_specs=(pl.BlockSpec(memory_space=pltpu.VMEM),) * 4,
        scratch_shapes=[
            vmem(NZ, WIDE, NY), vmem(NZ, WIDE, NY),
            vmem(NZ + 2, NX, NY),
            vmem(*full), vmem(*full), vmem(*full), vmem(*full), vmem(*full),
            vmem(*plane), vmem(*plane), vmem(*plane), vmem(*plane),
            vmem(2, *plane), vmem(2, *plane), vmem(*plane), vmem(*plane),
            vmem(4, NZ, NY),
            vmem(4, *plane), vmem(2, 4, NZ, NY),
            vmem(SUBSTEPS, 2, 2, *plane), vmem(SUBSTEPS, 2, 4, NZ, NY),
            vmem(2, *plane), vmem(2, 8, NY), vmem(2, *plane),
            vmem(3, *plane), vmem(LEVS, 3, *plane),
            vmem(5, *plane), vmem(SUBSTEPS, 3, 2, *plane), vmem(17, *plane),
            vmem(NZ + 2, NX, NY), vmem(NZ + 2, NX, NY), vmem(*full), vmem(*full),
            vmem(4, 2, *plane), vmem(*plane), vmem(2, *plane), vmem(2, 2, *plane),
            pltpu.VMEM((2 * NY, NY), BF16), vmem(*full),
            vmem(2, 12, NZ, NY), vmem(8, NZ, NY), vmem(2, *plane),
            dma(8),
            dma(4), dma(SUBSTEPS, 4), dma(3), dma(3), dma(3), dma(SUBSTEPS, 3),
            dma(4), dma(4), dma(2), dma(2),
        ],
        compiler_params=pltpu.CompilerParams(
            collective_id=0, has_side_effects=True, vmem_limit_bytes=53000 * 1024
        ),
    )(*blocks[:4], jnp.stack(blocks[4:7]), blocks[7])
    return pl.pallas_call(
        store,
        out_shape=(whole,) * 4,
        in_specs=[anywhere] * 4,
        out_specs=(hbm,) * 4,
        scratch_shapes=[dma(4)],
        compiler_params=pltpu.CompilerParams(vmem_limit_bytes=1024 * 1024),
        cost_estimate=pl.CostEstimate(flops=0, bytes_accessed=4_000_000, transcendentals=0),
    )(*blocks)


def solution(mesh):
    field, column = P("lev", "gx", "gy"), P("gx", "gy")
    return jax.shard_map(
        local,
        mesh=mesh,
        in_specs=(field, field, field, field, column, column, column, field),
        out_specs=(field, field, field, field),
        check_vma=False,
    )
```

```python
import jax
import jax.numpy as jnp
from jax import lax
from jax.experimental import pallas as pl
from jax.experimental.pallas import tpu as pltpu
from jax.sharding import PartitionSpec as P

SUBSTEPS = 2
GRAD = 0.35 / 12.0
VERT = 0.25

NZ, NX, NY = 32, 32, 128
GAP = 8
WIDE = NX + 2 * GAP
LEVS = 4
UNROLL = 8
F32 = jnp.float32
BF16 = jnp.bfloat16
CHUNK = 4
EDGE_ROWS = (0, 1, 2, 3, NX - 4, NX - 3, NX - 2, NX - 1)
FLUX_ROWS = (0, 1, NX - 2, NX - 1)


def level_rows(ref, row, first=0):
    levels, rows, lanes = ref.shape
    return ref.reshape(levels * rows, lanes), pl.ds(first * rows + row, NZ, stride=rows)


def get_rows(ref, row, first=0):
    flat, there = level_rows(ref, row, first)
    return flat[there, :]


def set_rows(ref, row, value, first=0):
    flat, there = level_rows(ref, row, first)
    flat[there, :] = value


def kernel(
    wx_h, wy_h, wz_h, p_h, j_h, sx_h, sy_h, st_h,
    wx, wy, wz, pout,
    pbuf, fbuf, ps, st, inv, up_s, q_s, val,
    jac, ijac, slx, sly,
    wyp, npk, jpk, ijpk, nrow,
    ymsg, xmsg, yrecv, xrecv, jprecv, jrecv, strecv,
    vset, vsetrecv, vmsg, vrecv, coef,
    pt, qt, pd, qd, wpk, slypk, gsum, dpk, dmat, p_s, xw, dpx, farp,
    load_sem,
    hs_send, hs_recv, ss_send, ss_recv, vs_send, vs_recv, js_send, js_recv, es_send, es_recv,
):
    gx, gy, lev = lax.axis_index("gx"), lax.axis_index("gy"), lax.axis_index("lev")
    ngx, ngy = lax.axis_size("gx"), lax.axis_size("gy")
    xlo, xhi = lax.rem(gx + ngx - 1, ngx), lax.rem(gx + 1, ngx)
    ylo, yhi = lax.rem(gy + ngy - 1, ngy), lax.rem(gy + 1, ngy)
    up, down, over = lax.rem(lev + 1, LEVS), lax.rem(lev + 3, LEVS), lax.rem(lev + 2, LEVS)
    mesh_id = pl.DeviceIdType.MESH

    def remote(src, dst, send, recv, where):
        return pltpu.make_async_remote_copy(
            src_ref=src, dst_ref=dst, send_sem=send, recv_sem=recv,
            device_id=where, device_id_type=mesh_id,
        )

    loads = [
        pltpu.make_async_copy(src, dst, load_sem.at[i])
        for i, (src, dst) in enumerate((
            (p_h, pbuf.at[:, GAP:GAP + NX, :]), (wy_h, wy), (wx_h, wx), (j_h, jac),
            (st_h, st), (sx_h, slx), (sy_h, sly), (wz_h, wz),
        ))
    ]
    barrier = pltpu.get_barrier_semaphore()
    partners = (
        {"gx": xlo}, {"gx": xhi}, {"gy": ylo}, {"gy": yhi},
        {"lev": up}, {"lev": down}, {"lev": over},
    )
    for where in partners:
        pl.semaphore_signal(barrier, inc=1, device_id=where, device_id_type=mesh_id)
    for copy in loads:
        copy.start()

    gap = jnp.zeros((GAP, NY), F32)

    def clear(l, carry):
        pbuf[l, 0:GAP, :] = gap
        pbuf[l, GAP + NX:WIDE, :] = gap
        fbuf[l, 0:GAP, :] = gap
        fbuf[l, GAP + NX:WIDE, :] = gap
        return carry

    lax.fori_loop(0, NZ, clear, 0, unroll=UNROLL)
    ps[0] = jnp.zeros((NX, NY), F32)
    ps[NZ + 1] = jnp.zeros((NX, NY), F32)

    lane = lax.broadcasted_iota(jnp.int32, (1, NY), 1)
    pos, group = lane & 7, lane >> 3

    def at(value, *places):
        hit = pos == places[0]
        for place in places[1:]:
            hit = hit | (pos == place)
        return jnp.where(hit, F32(value), F32(0))

    own_taps = (
        (2, at(1.0, 2, 3, 6, 7)), (1, at(-8.0, 1, 2, 3, 5, 6, 7)),
        (NY - 1, at(8.0, 0, 1, 2, 4, 5, 6)), (NY - 2, at(-1.0, 0, 1, 4, 5)),
    )
    far_taps = (
        (2, at(1.0, 4, 5)), (1, at(-8.0, 4)), (NY - 1, at(8.0, 3)), (NY - 2, at(-1.0, 2, 3)),
    )

    flux_taps = (
        (2, at(1.0, 4, 5), at(1.0, 2, 3)), (1, at(-8.0, 2, 4, 5), at(-8.0, 3)),
        (NY - 1, at(8.0, 2, 3, 5), at(8.0, 4)), (NY - 2, at(-1.0, 2, 3), at(-1.0, 4, 5)),
    )

    def taps(z, which):
        return sum(c * pltpu.roll(z, s, 1) for s, c in which)

    low_half, inner = pos < 4, (pos >= 2) & (pos <= 5)
    near_edge = (lane < 4) | (lane >= NY - 4)

    ahead = lax.broadcasted_iota(jnp.int32, (NY, NY), 0) - lax.broadcasted_iota(jnp.int32, (NY, NY), 1)
    band = jnp.zeros((NY, NY), F32)
    for k, c in ((-2, 1.0), (-1, -8.0), (1, 8.0), (2, -1.0)):
        band = jnp.where(ahead == k, F32(c), band)
    dmat[0:NY, :] = band.astype(BF16)
    dmat[NY:2 * NY, :] = band.astype(BF16)

    def lane_diff(f):
        flat = f.reshape(CHUNK * NX, NY)
        high = flat.astype(BF16)
        low = (flat - high.astype(F32)).astype(BF16)
        both = jnp.concatenate([high, low], axis=1)
        return jnp.dot(both, dmat[...], preferred_element_type=F32).reshape(CHUNK, NX, NY)

    acc0 = jnp.zeros((NX, NY), F32)
    def pack(sources):
        out = []
        for half in range(2):
            carry = [acc0] * len(sources)
            for i in range(16):
                here = group == i
                for k, src in enumerate(sources):
                    turned = pltpu.roll(src(half * 16 + i), (8 * i + 4) % NY, 1)
                    carry[k] = jnp.where(here, turned, carry[k])
            out.append(carry)
        return tuple(zip(*out))

    def spread_out(plane):
        z = jnp.where(lane < 8, pltpu.roll(plane, 4, 1), 0.0)
        for shift in (8, 16, 32, 64):
            z = z + pltpu.roll(z, shift, 1)
        return z

    def prow(r):
        return get_rows(pbuf, GAP + r)

    def jrow(r):
        return jac[r:r + 1, :]

    def y_copies(step):
        return (
            remote(ymsg.at[2:4], yrecv.at[step, 0], hs_send.at[0], hs_recv.at[step, 0], {"gy": yhi}),
            remote(ymsg.at[2:4], yrecv.at[step, 1], hs_send.at[1], hs_recv.at[step, 1], {"gy": ylo}),
        )

    def x_copies(step):
        return (
            remote(xmsg.at[1], xrecv.at[step, 0], hs_send.at[2], hs_recv.at[step, 2], {"gx": xhi}),
            remote(xmsg.at[0], xrecv.at[step, 1], hs_send.at[3], hs_recv.at[step, 3], {"gx": xlo}),
        )

    def edges_out(step):
        if step == 0:
            loads[0].wait()
            loads[2].wait()
            loads[3].wait()
        p0, p1, p2, p3 = (prow(r) for r in range(4))
        p28, p29, p30, p31 = (prow(r) for r in range(NX - 4, NX))
        wind_row = lambda i: nrow[i] if step else get_rows(wx, FLUX_ROWS[i])
        n0 = wind_row(0) - GRAD * (8.0 * p1 - p2)
        n1 = wind_row(1) - GRAD * (8.0 * (p2 - p0) - p3)
        n30 = wind_row(2) - GRAD * (p28 + 8.0 * (p31 - p29))
        n31 = wind_row(3) - GRAD * (p29 - 8.0 * p30)
        for i, n in enumerate((n0, n1, n30, n31)):
            nrow[i] = n
        xmsg[0, 0] = p0
        xmsg[0, 1] = p1
        xmsg[0, 2] = jrow(0) * n0
        xmsg[0, 3] = jrow(1) * n1
        xmsg[1, 0] = p30
        xmsg[1, 1] = p31
        xmsg[1, 2] = jrow(NX - 2) * n30
        xmsg[1, 3] = jrow(NX - 1) * n31
        if step == 0:
            pl.semaphore_wait(barrier, len(partners))
        for copy in x_copies(step):
            copy.start()
        if step == 0:
            columns()
        pressure = lambda l: pbuf[l, GAP:GAP + NX, :]
        if step == 0:
            jpk[...] = spread_out(jac[...])
            loads[1].wait()
            packed = pack((pressure, lambda l: wy[l]))
            for half in range(2):
                wyp[half] = packed[1][half]
        else:
            packed = pack((pressure,))
        for half in range(2):
            ymsg[half] = packed[0][half]
        jp = jpk[...]
        for half in range(2):
            pp = ymsg[half]
            n = wyp[half] - GRAD * taps(pp, own_taps)
            npk[half] = n
            flux = jp * n
            far = jnp.where(pos < 2, pltpu.roll(flux, NY - 2, 1), pltpu.roll(flux, 2, 1))
            ymsg[2 + half] = jnp.where(inner, pp, far)
        for copy in y_copies(step):
            copy.start()
        far_parts()

    def far_parts():
        for half in range(2):
            farp[half] = taps(ymsg[half], far_taps)

    def edges_in(step):
        for copy in y_copies(step):
            copy.wait()
        jp, ijp = jpk[...], ijpk[...]
        change = [acc0, acc0]
        jh = jnp.where(low_half, jprecv[0], jprecv[1])
        for half in range(2):
            m = jnp.where(low_half, yrecv[step, 0, half], yrecv[step, 1, half])
            turned = [pltpu.roll(m, k, 1) for k, _ in far_taps]
            d = -GRAD * sum(c * t for (_, c), t in zip(far_taps, turned))
            fh = jnp.where(low_half, turned[0], turned[3]) - GRAD * jh * farp[half]
            g = jp * d
            s = sum(
                pltpu.roll(jnp.where(inner, own * g + far * fh, 0.0), k, 1)
                for k, own, far in flux_taps
            )
            wyp[half] = npk[half] + d
            dp = (-GRAD) * ijp * s
            dpk[0, half], dpk[1, half] = d, dp
            sd = slypk[...] * d
            change = [c + wpk[k, half] * sd + wpk[k + 2, half] * dp for k, c in enumerate(change)]
        for side in range(2):
            total = change[side]
            for shift in (8, 16, 32, 64):
                total = total + pltpu.roll(total, shift, 1)
            gsum[side] = gsum[side] + jnp.where(near_edge, pltpu.roll(total, 124, 1), 0.0)
        unpack_level(0, 0, 124)
        unpack_level(1, 15, 4)

        for copy in x_copies(step):
            copy.wait()
        p0, p1, p30, p31 = (xmsg[0, 0], xmsg[0, 1], xmsg[1, 0], xmsg[1, 1])
        low, high = xrecv.at[step, 0], xrecv.at[step, 1]
        jm2, jm1 = jrecv[0, 6:7, :], jrecv[0, 7:8, :]
        j32, j33 = jrecv[1, 0:1, :], jrecv[1, 1:2, :]
        pm2, pm1, p32, p33 = low[0], low[1], high[0], high[1]
        d0 = -GRAD * (pm2 - 8.0 * pm1)
        d1 = -GRAD * pm1
        d30 = GRAD * p32
        d31 = -GRAD * (8.0 * p32 - p33)
        fm2 = low[2] + (GRAD * jm2) * p0
        fm1 = low[3] - (GRAD * jm1) * (8.0 * p0 - p1)
        f32 = high[2] - (GRAD * j32) * (p30 - 8.0 * p31)
        f33 = high[3] - (GRAD * j33) * p31
        g0, g1 = jrow(0) * d0, jrow(1) * d1
        g30, g31 = jrow(NX - 2) * d30, jrow(NX - 1) * d31
        delta = {0: d0, 1: d1, NX - 2: d30, NX - 1: d31}
        for i, r in enumerate(FLUX_ROWS):
            nrow[i] = nrow[i] + delta[r]
        sums = (
            fm2 + 8.0 * (g1 - fm1), fm1 - 8.0 * g0, g0 - 8.0 * g1, g1,
            -g30, 8.0 * g30 - g31, 8.0 * g31 - f32, 8.0 * (f32 - g30) - f33,
        )
        for i, (r, s) in enumerate(zip(EDGE_ROWS, sums)):
            dp = (-GRAD * ijac[r:r + 1, :]) * s
            dpx[i] = dp
            ps[1, r:r + 1, :] = ps[1, r:r + 1, :] + dp[0:1, :]
            ps[NZ, r:r + 1, :] = ps[NZ, r:r + 1, :] + dp[NZ - 1:NZ, :]
            for side in range(2):
                change = xw[side, i] * dp
                if r in delta:
                    change = change + xw[side, 8 + FLUX_ROWS.index(r)] * delta[r]
                gsum[side, r:r + 1, :] = gsum[side, r:r + 1, :] + jnp.sum(change, axis=0, keepdims=True)

    def unpack_level(half, i, shift):
        l = half * 16 + i
        wy[l] = wy[l] + jnp.where(near_edge, pltpu.roll(dpk[0, half], shift, 1), 0.0)
        ps[l + 1] = ps[l + 1] + jnp.where(near_edge, pltpu.roll(dpk[1, half], shift, 1), 0.0)

    def unpack_rest():
        for half in range(2):
            def unpack(i, carry):
                unpack_level(half, i, lax.rem(124 - 8 * i + NY, NY))
                return carry

            lax.fori_loop(1 - half, 16 - half, unpack, 0, unroll=5)

    def pre_source(l):
        return wz[l] + slx[...] * wx[l] + sly[...] * wy[l] - VERT * (ps[l + 2] - ps[l])

    def block_ends():
        def add(l, carry):
            rhs = pre_source(l)
            return carry[0] + pt[l + 1] * rhs, carry[1] + qt[l + 1] * rhs

        gsum[0], gsum[1] = lax.fori_loop(0, NZ, add, (acc0, acc0), unroll=UNROLL)

    def local_step():
        def row_diff(ref, lv):
            at_row = lambda k: ref[lv, GAP + k:GAP + NX + k, :]
            return (at_row(-2) - at_row(2)) + 8.0 * (at_row(1) - at_row(-1))

        def gradients(i, carry):
            lv = pl.ds(i * CHUNK, CHUNK)
            nx = wx[lv] - GRAD * row_diff(pbuf, lv)
            wx[lv] = nx
            fbuf[lv, GAP:GAP + NX, :] = jac[...] * nx
            wy[lv] = wy[lv] - GRAD * lane_diff(pbuf[lv, GAP:GAP + NX, :])
            return carry

        lax.fori_loop(0, NZ // CHUNK, gradients, 0, unroll=2)

        def divergence(i, carry):
            lv = pl.ds(i * CHUNK, CHUNK)
            spread = row_diff(fbuf, lv) + lane_diff(jac[...] * wy[lv])
            ps[pl.ds(i * CHUNK + 1, CHUNK)] = pbuf[lv, GAP:GAP + NX, :] - (GRAD * ijac[...]) * spread
            return carry

        lax.fori_loop(0, NZ // CHUNK, divergence, 0, unroll=2)

    jac_copies = (
        remote(jpk, jprecv.at[0], js_send.at[0], js_recv.at[0], {"gy": yhi}),
        remote(jpk, jprecv.at[1], js_send.at[1], js_recv.at[1], {"gy": ylo}),
        remote(jac.at[NX - 8:NX], jrecv.at[0], js_send.at[2], js_recv.at[2], {"gx": xhi}),
        remote(jac.at[0:8], jrecv.at[1], js_send.at[3], js_recv.at[3], {"gx": xlo}),
    )
    stiff_copies = (
        remote(st.at[NZ - 1], strecv.at[0], es_send.at[0], es_recv.at[0], {"lev": up}),
        remote(st.at[0], strecv.at[1], es_send.at[1], es_recv.at[1], {"lev": down}),
    )
    set_copies = (
        remote(vset, vsetrecv.at[lev], ss_send.at[0], ss_recv.at[0], {"lev": up}),
        remote(vset, vsetrecv.at[lev], ss_send.at[1], ss_recv.at[1], {"lev": down}),
        remote(vset, vsetrecv.at[lev], ss_send.at[2], ss_recv.at[2], {"lev": over}),
    )
    set_arrivals = (
        remote(vset, vsetrecv.at[down], ss_send.at[0], ss_recv.at[0], {"lev": up}),
        remote(vset, vsetrecv.at[up], ss_send.at[1], ss_recv.at[1], {"lev": down}),
        remote(vset, vsetrecv.at[over], ss_send.at[2], ss_recv.at[2], {"lev": over}),
    )

    def v_copies(step):
        return (
            remote(vmsg.at[3:5], vrecv.at[step, 0], vs_send.at[0], vs_recv.at[step, 0], {"lev": up}),
            remote(vmsg.at[0:2], vrecv.at[step, 1], vs_send.at[1], vs_recv.at[step, 1], {"lev": down}),
            remote(vmsg.at[2:3], vrecv.at[step, 2, 0:1], vs_send.at[2], vs_recv.at[step, 2], {"lev": over}),
        )

    def columns():
        loads[4].wait()
        for copy in stiff_copies:
            copy.start()

        def factor(i, carry):
            rising, falling = carry
            h = NZ - 1 - i
            inv_l, inv_h = 1.0 / st[i], 1.0 / st[h]
            rising = 1.0 / (2.0 + inv_l - rising)
            falling = 1.0 / (2.0 + inv_h - falling)
            up_s[i] = rising
            val[h] = falling
            return rising, falling

        lax.fori_loop(0, NZ, factor, (acc0, acc0), unroll=UNROLL)

        def spikes(i, carry):
            below, above = carry
            h = NZ - 1 - i
            below = below * val[i]
            above = above * up_s[h]
            p_s[i] = below
            q_s[h] = above
            inv[i] = 1.0 / st[i]
            return below, above

        ones = jnp.ones((NX, NY), F32)
        lax.fori_loop(0, NZ, spikes, (ones, ones), unroll=UNROLL)
        vset[0] = p_s[0]
        vset[1] = q_s[0]
        vset[2] = q_s[NZ - 1]
        for copy in set_copies:
            copy.start()

    edges_out(0)
    for copy in jac_copies:
        copy.start()

    pt[0] = qt[0] = pt[NZ + 1] = qt[NZ + 1] = acc0

    def weigh(l, carry):
        pt[l + 1] = p_s[l] * inv[l]
        qt[l + 1] = q_s[l] * inv[l]
        return carry

    lax.fori_loop(0, NZ, weigh, 0, unroll=UNROLL)

    def weigh_apart(l, carry):
        pd[l] = VERT * (pt[l + 2] - pt[l])
        qd[l] = VERT * (qt[l + 2] - qt[l])
        return carry

    lax.fori_loop(0, NZ, weigh_apart, 0, unroll=UNROLL)
    ijac[...] = 1.0 / jac[...]
    ijpk[...] = 1.0 / jpk[...]
    for copy in loads[5:]:
        copy.wait()
    slypk[...] = spread_out(sly[...])

    depth = lax.broadcasted_iota(jnp.int32, (NZ, NY), 0)
    inside = (depth > 0) & (depth < NZ - 1)

    def pick(*values):
        out = values[-1]
        for i in range(LEVS - 2, -1, -1):
            out = jnp.where(lev == i, values[i], out)
        return out

    def after_setup():
        for copy in set_copies:
            copy.wait_send()
        for copy in set_arrivals:
            copy.wait_recv()
        vsetrecv[lev] = vset[...]
        pa = [vsetrecv[i, 0] for i in range(LEVS)]
        qa = [vsetrecv[i, 1] for i in range(LEVS)]
        qb = [vsetrecv[i, 2] for i in range(LEVS)]
        b0 = qb[0]
        t1 = qa[1] / (1.0 - b0 * pa[1])
        b1 = qb[1] + t1 * b0 * qa[1]
        t2 = qa[2] / (1.0 - b1 * pa[2])
        b2 = qb[2] + t2 * b1 * qa[2]
        e3 = pa[3]
        r2 = qa[2] / (1.0 - e3 * qb[2])
        e2 = pa[2] + r2 * e3 * qa[2]
        r1 = qa[1] / (1.0 - e2 * qb[1])
        e1 = pa[1] + r1 * e2 * qa[1]
        z0 = 1.0 / (1.0 - b0 * e1)
        z1 = 1.0 / (1.0 - b1 * e2)
        z2 = 1.0 / (1.0 - b2 * e3)
        for i, c in enumerate((t1, b0, b1, t2, r1, r2, e2, e3, e1, b2, z0, z1, z2)):
            coef[i] = c
        coef[15] = pick(acc0, t1 * b0, t2 * b1, acc0)
        coef[16] = pick(acc0, r1 * e2, r2 * e3, acc0)

    for step in range(SUBSTEPS):
        last = step == SUBSTEPS - 1
        if step > 0:
            edges_out(step)
        local_step()
        block_ends()
        if step == 0:
            packed = pack((lambda l: pt[l + 1], lambda l: qt[l + 1], lambda l: pd[l], lambda l: qd[l]))
            for k in range(4):
                for half in range(2):
                    wpk[k, half] = packed[k][half]
            for side, (near, far) in enumerate(((pt, pd), (qt, qd))):
                for i, r in enumerate(EDGE_ROWS):
                    xw[side, i] = get_rows(far, r)
                for i, r in enumerate(FLUX_ROWS):
                    xw[side, 8 + i] = slx[r:r + 1, :] * get_rows(near, r, 1)
            for copy in jac_copies + stiff_copies:
                copy.wait()
            coef[13] = 1.0 / strecv[0]
            coef[14] = 1.0 / strecv[1]
            after_setup()
        edges_in(step)
        ga = gsum[0] - VERT * ps[1] * coef[13]
        gb = gsum[1] + VERT * ps[NZ] * coef[14]
        own_mu = gb + coef[15] * ga
        own_nu = ga + coef[16] * gb
        vmsg[0] = ps[1]
        vmsg[1] = jnp.where(lev == 0, own_mu, own_nu)
        vmsg[2] = jnp.where(lev < 2, own_mu, own_nu)
        vmsg[3] = jnp.where(lev == LEVS - 1, own_nu, own_mu)
        vmsg[4] = ps[NZ]
        for copy in v_copies(step):
            copy.start()
        gsum[0], gsum[1] = own_mu, own_nu
        for i, r in enumerate(FLUX_ROWS):
            set_rows(wx, r, nrow[i])
        for i, r in enumerate(EDGE_ROWS):
            there = dpx[i]
            set_rows(ps, r, get_rows(ps, r, 1) + jnp.where(inside, there, 0.0), 1)
        unpack_rest()

        def rising(l, v):
            v = (pre_source(l) * inv[l] + v) * up_s[l]
            val[l] = v
            return v

        top = lax.fori_loop(0, NZ, rising, acc0, unroll=UNROLL)

        def falling(i, x):
            l = NZ - 2 - i
            x = val[l] + up_s[l] * x
            val[l] = x
            return x

        lax.fori_loop(0, NZ - 1, falling, top, unroll=UNROLL)
        for copy in v_copies(step):
            copy.wait()
        own_mu, own_nu = gsum[0], gsum[1]
        low, high, far = vrecv[step, 0, 0], vrecv[step, 1, 1], vrecv[step, 2, 0]
        t1, b0, b1, t2, r1, r2, e2, e3, e1, b2, z0, z1, z2 = (coef[i] for i in range(13))
        a0 = pick(own_mu, low, far, high)
        a1 = pick(acc0, own_mu, low, far) + t1 * a0
        a2 = pick(acc0, acc0, own_mu, low) + t2 * a1
        c3 = pick(low, far, high, own_nu)
        c2 = pick(far, high, own_nu, acc0) + r2 * c3
        c1 = pick(high, own_nu, acc0, acc0) + r1 * c2
        w = pick(acc0, (a0 + b0 * c1) * z0, (a1 + b1 * c2) * z1, (a2 + b2 * c3) * z2)
        y = pick((c1 + e1 * a0) * z0, (c2 + e2 * a1) * z1, (c3 + e3 * a2) * z2, acc0)
        under = jnp.where(lev == 0, acc0, w - VERT * vrecv[step, 0, 1] * inv[0])
        above = jnp.where(lev == LEVS - 1, acc0, y + VERT * vrecv[step, 1, 0] * inv[NZ - 1])

        def solved(l):
            return val[l] + p_s[l] * w + q_s[l] * y

        def keep_pressure(l, p):
            if last:
                pout[l] = p
            else:
                pbuf[l, GAP:GAP + NX, :] = p

        def finish(l, carry):
            before, here = carry
            after = solved(l + 1)
            wz[l] = here
            keep_pressure(l, ps[l + 1] - VERT * (after - before))
            return here, after

        before, here = lax.fori_loop(0, NZ - 1, finish, (under, solved(0)), unroll=UNROLL)
        wz[NZ - 1] = here
        keep_pressure(NZ - 1, ps[NZ] - VERT * (above - before))


def store(*refs):
    sems = refs[-1]
    copies = [pltpu.make_async_copy(refs[i], refs[4 + i], sems.at[i]) for i in range(4)]
    for copy in copies:
        copy.start()
    for copy in copies:
        copy.wait()


def local(*blocks):
    whole = jax.ShapeDtypeStruct((NZ, NX, NY), F32)
    anywhere, hbm = pl.BlockSpec(memory_space=pl.ANY), pl.BlockSpec(memory_space=pltpu.HBM)

    def vmem(*shape):
        return pltpu.VMEM(shape, F32)

    def dma(*shape):
        return pltpu.SemaphoreType.DMA(shape)

    full, plane = (NZ, NX, NY), (NX, NY)
    blocks = pl.pallas_call(
        kernel,
        out_shape=(whole,) * 4,
        in_specs=[hbm] * 8,
        out_specs=(pl.BlockSpec(memory_space=pltpu.VMEM),) * 4,
        scratch_shapes=[
            vmem(NZ, WIDE, NY), vmem(NZ, WIDE, NY),
            vmem(NZ + 2, NX, NY),
            vmem(*full), vmem(*full), vmem(*full), vmem(*full), vmem(*full),
            vmem(*plane), vmem(*plane), vmem(*plane), vmem(*plane),
            vmem(2, *plane), vmem(2, *plane), vmem(*plane), vmem(*plane),
            vmem(4, NZ, NY),
            vmem(4, *plane), vmem(2, 4, NZ, NY),
            vmem(SUBSTEPS, 2, 2, *plane), vmem(SUBSTEPS, 2, 4, NZ, NY),
            vmem(2, *plane), vmem(2, 8, NY), vmem(2, *plane),
            vmem(3, *plane), vmem(LEVS, 3, *plane),
            vmem(5, *plane), vmem(SUBSTEPS, 3, 2, *plane), vmem(17, *plane),
            vmem(NZ + 2, NX, NY), vmem(NZ + 2, NX, NY), vmem(*full), vmem(*full),
            vmem(4, 2, *plane), vmem(*plane), vmem(2, *plane), vmem(2, 2, *plane),
            pltpu.VMEM((2 * NY, NY), BF16), vmem(*full),
            vmem(2, 12, NZ, NY), vmem(8, NZ, NY), vmem(2, *plane),
            dma(8),
            dma(4), dma(SUBSTEPS, 4), dma(3), dma(3), dma(3), dma(SUBSTEPS, 3),
            dma(4), dma(4), dma(2), dma(2),
        ],
        compiler_params=pltpu.CompilerParams(
            collective_id=0, has_side_effects=True, vmem_limit_bytes=40 * 1024 * 1024
        ),
    )(*[pltpu.with_memory_space_constraint(b, pltpu.HBM) for b in blocks])
    return pl.pallas_call(
        store,
        out_shape=(whole,) * 4,
        in_specs=[anywhere] * 4,
        out_specs=(hbm,) * 4,
        scratch_shapes=[dma(4)],
        compiler_params=pltpu.CompilerParams(vmem_limit_bytes=1024 * 1024),
        cost_estimate=pl.CostEstimate(flops=0, bytes_accessed=4_000_000, transcendentals=0),
    )(*blocks)


def solution(mesh):
    field, column = P("lev", "gx", "gy"), P("gx", "gy")
    return jax.shard_map(
        local,
        mesh=mesh,
        in_specs=(field, field, field, field, column, column, column, field),
        out_specs=(field, field, field, field),
        check_vma=False,
    )
```

```python
import jax
import jax.numpy as jnp
from jax import lax
from jax.experimental import pallas as pl
from jax.experimental.pallas import tpu as pltpu
from jax.sharding import PartitionSpec as P

SUBSTEPS = 2
GRAD = 0.35 / 12.0
VERT = 0.25

NZ, NX, NY = 32, 32, 128
GAP = 8
WIDE = NX + 2 * GAP
LEVS = 4
UNROLL = 8
F32 = jnp.float32
BF16 = jnp.bfloat16
CHUNK = 4
EDGE_ROWS = (0, 1, 2, 3, NX - 4, NX - 3, NX - 2, NX - 1)
FLUX_ROWS = (0, 1, NX - 2, NX - 1)


def level_rows(ref, row, first=0):
    levels, rows, lanes = ref.shape
    return ref.reshape(levels * rows, lanes), pl.ds(first * rows + row, NZ, stride=rows)


def get_rows(ref, row, first=0):
    flat, there = level_rows(ref, row, first)
    return flat[there, :]


def set_rows(ref, row, value, first=0):
    flat, there = level_rows(ref, row, first)
    flat[there, :] = value


def kernel(
    wx_h, wy_h, wz_h, p_h, j_h, sx_h, sy_h, st_h,
    wx, wy, wz, pout,
    pbuf, fbuf, ps, st, inv, up_s, q_s, val,
    jac, ijac, slx, sly,
    wyp, npk, jpk, ijpk, nrow,
    ymsg, xmsg, yrecv, xrecv, jprecv, jrecv, strecv,
    vset, vsetrecv, vmsg, vrecv, coef,
    pt, qt, pd, qd, wpk, slypk, gsum, dpk, dmat, p_s, xw, dpx, farp, erow, ends,
    load_sem,
    hs_send, hs_recv, ss_send, ss_recv, vs_send, vs_recv, js_send, js_recv, es_send, es_recv,
):
    gx, gy, lev = lax.axis_index("gx"), lax.axis_index("gy"), lax.axis_index("lev")
    ngx, ngy = lax.axis_size("gx"), lax.axis_size("gy")
    xlo, xhi = lax.rem(gx + ngx - 1, ngx), lax.rem(gx + 1, ngx)
    ylo, yhi = lax.rem(gy + ngy - 1, ngy), lax.rem(gy + 1, ngy)
    up, down, over = lax.rem(lev + 1, LEVS), lax.rem(lev + 3, LEVS), lax.rem(lev + 2, LEVS)
    mesh_id = pl.DeviceIdType.MESH

    def remote(src, dst, send, recv, where):
        return pltpu.make_async_remote_copy(
            src_ref=src, dst_ref=dst, send_sem=send, recv_sem=recv,
            device_id=where, device_id_type=mesh_id,
        )

    loads = [
        pltpu.make_async_copy(src, dst, load_sem.at[i])
        for i, (src, dst) in enumerate((
            (p_h, pbuf.at[:, GAP:GAP + NX, :]), (wy_h, wy), (wx_h, wx), (j_h, jac),
            (st_h, st), (sx_h, slx), (sy_h, sly), (wz_h, wz),
        ))
    ]
    barrier = pltpu.get_barrier_semaphore()
    partners = (
        {"gx": xlo}, {"gx": xhi}, {"gy": ylo}, {"gy": yhi},
        {"lev": up}, {"lev": down}, {"lev": over},
    )
    for where in partners:
        pl.semaphore_signal(barrier, inc=1, device_id=where, device_id_type=mesh_id)
    for copy in loads:
        copy.start()

    gap = jnp.zeros((GAP, NY), F32)

    def clear(l, carry):
        pbuf[l, 0:GAP, :] = gap
        pbuf[l, GAP + NX:WIDE, :] = gap
        fbuf[l, 0:GAP, :] = gap
        fbuf[l, GAP + NX:WIDE, :] = gap
        return carry

    lax.fori_loop(0, NZ, clear, 0, unroll=UNROLL)
    ps[0] = jnp.zeros((NX, NY), F32)
    ps[NZ + 1] = jnp.zeros((NX, NY), F32)

    lane = lax.broadcasted_iota(jnp.int32, (1, NY), 1)
    pos, group = lane & 7, lane >> 3

    def at(value, *places):
        hit = pos == places[0]
        for place in places[1:]:
            hit = hit | (pos == place)
        return jnp.where(hit, F32(value), F32(0))

    own_taps = (
        (2, at(1.0, 2, 3, 6, 7)), (1, at(-8.0, 1, 2, 3, 5, 6, 7)),
        (NY - 1, at(8.0, 0, 1, 2, 4, 5, 6)), (NY - 2, at(-1.0, 0, 1, 4, 5)),
    )
    far_taps = (
        (2, at(1.0, 4, 5)), (1, at(-8.0, 4)), (NY - 1, at(8.0, 3)), (NY - 2, at(-1.0, 2, 3)),
    )

    flux_taps = (
        (2, at(1.0, 4, 5), at(1.0, 2, 3)), (1, at(-8.0, 2, 4, 5), at(-8.0, 3)),
        (NY - 1, at(8.0, 2, 3, 5), at(8.0, 4)), (NY - 2, at(-1.0, 2, 3), at(-1.0, 4, 5)),
    )

    def taps(z, which):
        return sum(c * pltpu.roll(z, s, 1) for s, c in which)

    low_half, inner = pos < 4, (pos >= 2) & (pos <= 5)
    near_edge = (lane < 4) | (lane >= NY - 4)

    ahead = lax.broadcasted_iota(jnp.int32, (NY, NY), 0) - lax.broadcasted_iota(jnp.int32, (NY, NY), 1)
    band = jnp.zeros((NY, NY), F32)
    for k, c in ((-2, 1.0), (-1, -8.0), (1, 8.0), (2, -1.0)):
        band = jnp.where(ahead == k, F32(c), band)
    dmat[0:NY, :] = band.astype(BF16)
    dmat[NY:2 * NY, :] = band.astype(BF16)

    def lane_diff(f):
        flat = f.reshape(CHUNK * NX, NY)
        high = flat.astype(BF16)
        low = (flat - high.astype(F32)).astype(BF16)
        both = jnp.concatenate([high, low], axis=1)
        return jnp.dot(both, dmat[...], preferred_element_type=F32).reshape(CHUNK, NX, NY)

    acc0 = jnp.zeros((NX, NY), F32)
    def pack(sources):
        out = []
        for half in range(2):
            carry = [acc0] * len(sources)
            for i in range(16):
                here = group == i
                for k, src in enumerate(sources):
                    turned = pltpu.roll(src(half * 16 + i), (8 * i + 4) % NY, 1)
                    carry[k] = jnp.where(here, turned, carry[k])
            out.append(carry)
        return tuple(zip(*out))

    def spread_out(plane):
        z = jnp.where(lane < 8, pltpu.roll(plane, 4, 1), 0.0)
        for shift in (8, 16, 32, 64):
            z = z + pltpu.roll(z, shift, 1)
        return z

    def prow(r):
        return get_rows(pbuf, GAP + r)

    def jrow(r):
        return jac[r:r + 1, :]

    def y_copies(step):
        return (
            remote(ymsg.at[2:4], yrecv.at[step, 0], hs_send.at[0], hs_recv.at[step, 0], {"gy": yhi}),
            remote(ymsg.at[2:4], yrecv.at[step, 1], hs_send.at[1], hs_recv.at[step, 1], {"gy": ylo}),
        )

    def x_copies(step):
        return (
            remote(xmsg.at[1], xrecv.at[step, 0], hs_send.at[2], hs_recv.at[step, 2], {"gx": xhi}),
            remote(xmsg.at[0], xrecv.at[step, 1], hs_send.at[3], hs_recv.at[step, 3], {"gx": xlo}),
        )

    def rows_out(step, rows):
        if step == 0:
            loads[0].wait()
            loads[2].wait()
            loads[3].wait()
        p0, p1, p2, p3, p28, p29, p30, p31 = rows()
        wind_row = lambda i: nrow[i] if step else get_rows(wx, FLUX_ROWS[i])
        n0 = wind_row(0) - GRAD * (8.0 * p1 - p2)
        n1 = wind_row(1) - GRAD * (8.0 * (p2 - p0) - p3)
        n30 = wind_row(2) - GRAD * (p28 + 8.0 * (p31 - p29))
        n31 = wind_row(3) - GRAD * (p29 - 8.0 * p30)
        for i, n in enumerate((n0, n1, n30, n31)):
            nrow[i] = n
        xmsg[0, 0] = p0
        xmsg[0, 1] = p1
        xmsg[0, 2] = jrow(0) * n0
        xmsg[0, 3] = jrow(1) * n1
        xmsg[1, 0] = p30
        xmsg[1, 1] = p31
        xmsg[1, 2] = jrow(NX - 2) * n30
        xmsg[1, 3] = jrow(NX - 1) * n31
        if step == 0:
            pl.semaphore_wait(barrier, len(partners))
        for copy in x_copies(step):
            copy.start()
        if step == 0:
            columns()

    def columns_out(step):
        pressure = lambda l: pbuf[l, GAP:GAP + NX, :]
        if step == 0:
            jpk[...] = spread_out(jac[...])
            loads[1].wait()
            packed = pack((pressure, lambda l: wy[l]))
            for half in range(2):
                wyp[half] = packed[1][half]
        else:
            packed = pack((pressure,))
        for half in range(2):
            ymsg[half] = packed[0][half]
        jp = jpk[...]
        for half in range(2):
            pp = ymsg[half]
            n = wyp[half] - GRAD * taps(pp, own_taps)
            npk[half] = n
            flux = jp * n
            far = jnp.where(pos < 2, pltpu.roll(flux, NY - 2, 1), pltpu.roll(flux, 2, 1))
            ymsg[2 + half] = jnp.where(inner, pp, far)
        for copy in y_copies(step):
            copy.start()
        far_parts()

    def far_parts():
        for half in range(2):
            farp[half] = taps(ymsg[half], far_taps)

    def edges_in(step):
        for copy in y_copies(step):
            copy.wait()
        jp, ijp = jpk[...], ijpk[...]
        change = [acc0, acc0]
        jh = jnp.where(low_half, jprecv[0], jprecv[1])
        for half in range(2):
            m = jnp.where(low_half, yrecv[step, 0, half], yrecv[step, 1, half])
            turned = [pltpu.roll(m, k, 1) for k, _ in far_taps]
            d = -GRAD * sum(c * t for (_, c), t in zip(far_taps, turned))
            fh = jnp.where(low_half, turned[0], turned[3]) - GRAD * jh * farp[half]
            g = jp * d
            s = sum(
                pltpu.roll(jnp.where(inner, own * g + far * fh, 0.0), k, 1)
                for k, own, far in flux_taps
            )
            wyp[half] = npk[half] + d
            dp = (-GRAD) * ijp * s
            dpk[0, half], dpk[1, half] = d, dp
            sd = slypk[...] * d
            change = [c + wpk[k, half] * sd + wpk[k + 2, half] * dp for k, c in enumerate(change)]
        for side in range(2):
            total = change[side]
            for shift in (8, 16, 32, 64):
                total = total + pltpu.roll(total, shift, 1)
            gsum[side] = gsum[side] + jnp.where(near_edge, pltpu.roll(total, 124, 1), 0.0)
        unpack_level(0, 0, 124)
        unpack_level(1, 15, 4)

        for copy in x_copies(step):
            copy.wait()
        p0, p1, p30, p31 = (xmsg[0, 0], xmsg[0, 1], xmsg[1, 0], xmsg[1, 1])
        low, high = xrecv.at[step, 0], xrecv.at[step, 1]
        jm2, jm1 = jrecv[0, 6:7, :], jrecv[0, 7:8, :]
        j32, j33 = jrecv[1, 0:1, :], jrecv[1, 1:2, :]
        pm2, pm1, p32, p33 = low[0], low[1], high[0], high[1]
        d0 = -GRAD * (pm2 - 8.0 * pm1)
        d1 = -GRAD * pm1
        d30 = GRAD * p32
        d31 = -GRAD * (8.0 * p32 - p33)
        fm2 = low[2] + (GRAD * jm2) * p0
        fm1 = low[3] - (GRAD * jm1) * (8.0 * p0 - p1)
        f32 = high[2] - (GRAD * j32) * (p30 - 8.0 * p31)
        f33 = high[3] - (GRAD * j33) * p31
        g0, g1 = jrow(0) * d0, jrow(1) * d1
        g30, g31 = jrow(NX - 2) * d30, jrow(NX - 1) * d31
        delta = {0: d0, 1: d1, NX - 2: d30, NX - 1: d31}
        for i, r in enumerate(FLUX_ROWS):
            nrow[i] = nrow[i] + delta[r]
        sums = (
            fm2 + 8.0 * (g1 - fm1), fm1 - 8.0 * g0, g0 - 8.0 * g1, g1,
            -g30, 8.0 * g30 - g31, 8.0 * g31 - f32, 8.0 * (f32 - g30) - f33,
        )
        for i, (r, s) in enumerate(zip(EDGE_ROWS, sums)):
            dp = (-GRAD * ijac[r:r + 1, :]) * s
            dpx[i] = dp
            ps[1, r:r + 1, :] = ps[1, r:r + 1, :] + dp[0:1, :]
            ps[NZ, r:r + 1, :] = ps[NZ, r:r + 1, :] + dp[NZ - 1:NZ, :]
            for side in range(2):
                change = xw[side, i] * dp
                if r in delta:
                    change = change + xw[side, 8 + FLUX_ROWS.index(r)] * delta[r]
                gsum[side, r:r + 1, :] = gsum[side, r:r + 1, :] + jnp.sum(change, axis=0, keepdims=True)

    def unpack_level(half, i, shift):
        l = half * 16 + i
        wy[l] = wy[l] + jnp.where(near_edge, pltpu.roll(dpk[0, half], shift, 1), 0.0)
        ps[l + 1] = ps[l + 1] + jnp.where(near_edge, pltpu.roll(dpk[1, half], shift, 1), 0.0)

    def unpack_rest():
        for half in range(2):
            def unpack(i, carry):
                unpack_level(half, i, lax.rem(124 - 8 * i + NY, NY))
                return carry

            lax.fori_loop(1 - half, 16 - half, unpack, 0, unroll=5)

    def pre_source(l):
        return wz[l] + slx[...] * wx[l] + sly[...] * wy[l] - VERT * (ps[l + 2] - ps[l])

    def block_ends():
        def add(l, carry):
            rhs = pre_source(l)
            return carry[0] + pt[l + 1] * rhs, carry[1] + qt[l + 1] * rhs

        gsum[0], gsum[1] = lax.fori_loop(0, NZ, add, (acc0, acc0), unroll=UNROLL)

    def local_step():
        def row_diff(ref, lv):
            at_row = lambda k: ref[lv, GAP + k:GAP + NX + k, :]
            return (at_row(-2) - at_row(2)) + 8.0 * (at_row(1) - at_row(-1))

        def gradients(i, carry):
            lv = pl.ds(i * CHUNK, CHUNK)
            nx = wx[lv] - GRAD * row_diff(pbuf, lv)
            wx[lv] = nx
            fbuf[lv, GAP:GAP + NX, :] = jac[...] * nx
            wy[lv] = wy[lv] - GRAD * lane_diff(pbuf[lv, GAP:GAP + NX, :])
            return carry

        lax.fori_loop(0, NZ // CHUNK, gradients, 0, unroll=2)

        def divergence(i, carry):
            lv = pl.ds(i * CHUNK, CHUNK)
            spread = row_diff(fbuf, lv) + lane_diff(jac[...] * wy[lv])
            ps[pl.ds(i * CHUNK + 1, CHUNK)] = pbuf[lv, GAP:GAP + NX, :] - (GRAD * ijac[...]) * spread
            return carry

        lax.fori_loop(0, NZ // CHUNK, divergence, 0, unroll=2)

    jac_copies = (
        remote(jpk, jprecv.at[0], js_send.at[0], js_recv.at[0], {"gy": yhi}),
        remote(jpk, jprecv.at[1], js_send.at[1], js_recv.at[1], {"gy": ylo}),
        remote(jac.at[NX - 8:NX], jrecv.at[0], js_send.at[2], js_recv.at[2], {"gx": xhi}),
        remote(jac.at[0:8], jrecv.at[1], js_send.at[3], js_recv.at[3], {"gx": xlo}),
    )
    stiff_copies = (
        remote(st.at[NZ - 1], strecv.at[0], es_send.at[0], es_recv.at[0], {"lev": up}),
        remote(st.at[0], strecv.at[1], es_send.at[1], es_recv.at[1], {"lev": down}),
    )
    set_copies = (
        remote(vset, vsetrecv.at[lev], ss_send.at[0], ss_recv.at[0], {"lev": up}),
        remote(vset, vsetrecv.at[lev], ss_send.at[1], ss_recv.at[1], {"lev": down}),
        remote(vset, vsetrecv.at[lev], ss_send.at[2], ss_recv.at[2], {"lev": over}),
    )
    set_arrivals = (
        remote(vset, vsetrecv.at[down], ss_send.at[0], ss_recv.at[0], {"lev": up}),
        remote(vset, vsetrecv.at[up], ss_send.at[1], ss_recv.at[1], {"lev": down}),
        remote(vset, vsetrecv.at[over], ss_send.at[2], ss_recv.at[2], {"lev": over}),
    )

    def v_copies(step):
        return (
            remote(vmsg.at[3:5], vrecv.at[step, 0], vs_send.at[0], vs_recv.at[step, 0], {"lev": up}),
            remote(vmsg.at[0:2], vrecv.at[step, 1], vs_send.at[1], vs_recv.at[step, 1], {"lev": down}),
            remote(vmsg.at[2:3], vrecv.at[step, 2, 0:1], vs_send.at[2], vs_recv.at[step, 2], {"lev": over}),
        )

    def columns():
        loads[4].wait()
        for copy in stiff_copies:
            copy.start()

        def factor(i, carry):
            rising, falling = carry
            h = NZ - 1 - i
            inv_l, inv_h = 1.0 / st[i], 1.0 / st[h]
            rising = 1.0 / (2.0 + inv_l - rising)
            falling = 1.0 / (2.0 + inv_h - falling)
            up_s[i] = rising
            val[h] = falling
            return rising, falling

        lax.fori_loop(0, NZ, factor, (acc0, acc0), unroll=UNROLL)

        def spikes(i, carry):
            below, above = carry
            h = NZ - 1 - i
            below = below * val[i]
            above = above * up_s[h]
            p_s[i] = below
            q_s[h] = above
            inv[i] = 1.0 / st[i]
            return below, above

        ones = jnp.ones((NX, NY), F32)
        lax.fori_loop(0, NZ, spikes, (ones, ones), unroll=UNROLL)
        vset[0] = p_s[0]
        vset[1] = q_s[0]
        vset[2] = q_s[NZ - 1]
        for copy in set_copies:
            copy.start()

    rows_out(0, lambda: [prow(r) for r in EDGE_ROWS])
    columns_out(0)
    for copy in jac_copies:
        copy.start()

    pt[0] = qt[0] = pt[NZ + 1] = qt[NZ + 1] = acc0

    def weigh(l, carry):
        pt[l + 1] = p_s[l] * inv[l]
        qt[l + 1] = q_s[l] * inv[l]
        return carry

    lax.fori_loop(0, NZ, weigh, 0, unroll=UNROLL)

    def weigh_apart(l, carry):
        pd[l] = VERT * (pt[l + 2] - pt[l])
        qd[l] = VERT * (qt[l + 2] - qt[l])
        return carry

    lax.fori_loop(0, NZ, weigh_apart, 0, unroll=UNROLL)
    ijac[...] = 1.0 / jac[...]
    ijpk[...] = 1.0 / jpk[...]
    for copy in loads[5:]:
        copy.wait()
    slypk[...] = spread_out(sly[...])

    depth = lax.broadcasted_iota(jnp.int32, (NZ, NY), 0)
    inside = (depth > 0) & (depth < NZ - 1)

    def pick(*values):
        out = values[-1]
        for i in range(LEVS - 2, -1, -1):
            out = jnp.where(lev == i, values[i], out)
        return out

    def after_setup():
        for copy in set_copies:
            copy.wait_send()
        for copy in set_arrivals:
            copy.wait_recv()
        vsetrecv[lev] = vset[...]
        pa = [vsetrecv[i, 0] for i in range(LEVS)]
        qa = [vsetrecv[i, 1] for i in range(LEVS)]
        qb = [vsetrecv[i, 2] for i in range(LEVS)]
        b0 = qb[0]
        t1 = qa[1] / (1.0 - b0 * pa[1])
        b1 = qb[1] + t1 * b0 * qa[1]
        t2 = qa[2] / (1.0 - b1 * pa[2])
        b2 = qb[2] + t2 * b1 * qa[2]
        e3 = pa[3]
        r2 = qa[2] / (1.0 - e3 * qb[2])
        e2 = pa[2] + r2 * e3 * qa[2]
        r1 = qa[1] / (1.0 - e2 * qb[1])
        e1 = pa[1] + r1 * e2 * qa[1]
        z0 = 1.0 / (1.0 - b0 * e1)
        z1 = 1.0 / (1.0 - b1 * e2)
        z2 = 1.0 / (1.0 - b2 * e3)
        for i, c in enumerate((t1, b0, b1, t2, r1, r2, e2, e3, e1, b2, z0, z1, z2)):
            coef[i] = c
        coef[15] = pick(acc0, t1 * b0, t2 * b1, acc0)
        coef[16] = pick(acc0, r1 * e2, r2 * e3, acc0)

    for step in range(SUBSTEPS):
        last = step == SUBSTEPS - 1
        if step > 0:
            columns_out(step)
        local_step()
        block_ends()
        if step == 0:
            packed = pack((lambda l: pt[l + 1], lambda l: qt[l + 1], lambda l: pd[l], lambda l: qd[l]))
            for k in range(4):
                for half in range(2):
                    wpk[k, half] = packed[k][half]
            for side, (near, far) in enumerate(((pt, pd), (qt, qd))):
                for i, r in enumerate(EDGE_ROWS):
                    xw[side, i] = get_rows(far, r)
                for i, r in enumerate(FLUX_ROWS):
                    xw[side, 8 + i] = slx[r:r + 1, :] * get_rows(near, r, 1)
            for copy in jac_copies + stiff_copies:
                copy.wait()
            coef[13] = 1.0 / strecv[0]
            coef[14] = 1.0 / strecv[1]
            after_setup()
        edges_in(step)
        ga = gsum[0] - VERT * ps[1] * coef[13]
        gb = gsum[1] + VERT * ps[NZ] * coef[14]
        own_mu = gb + coef[15] * ga
        own_nu = ga + coef[16] * gb
        vmsg[0] = ps[1]
        vmsg[1] = jnp.where(lev == 0, own_mu, own_nu)
        vmsg[2] = jnp.where(lev < 2, own_mu, own_nu)
        vmsg[3] = jnp.where(lev == LEVS - 1, own_nu, own_mu)
        vmsg[4] = ps[NZ]
        for copy in v_copies(step):
            copy.start()
        gsum[0], gsum[1] = own_mu, own_nu
        for i, r in enumerate(FLUX_ROWS):
            set_rows(wx, r, nrow[i])
        for i, r in enumerate(EDGE_ROWS):
            there = dpx[i]
            set_rows(ps, r, get_rows(ps, r, 1) + jnp.where(inside, there, 0.0), 1)
        unpack_rest()

        def rising(l, v):
            v = (pre_source(l) * inv[l] + v) * up_s[l]
            val[l] = v
            return v

        top = lax.fori_loop(0, NZ, rising, acc0, unroll=UNROLL)

        def falling(i, x):
            l = NZ - 2 - i
            x = val[l] + up_s[l] * x
            val[l] = x
            return x

        lax.fori_loop(0, NZ - 1, falling, top, unroll=UNROLL)
        if not last:
            for i, r in enumerate(EDGE_ROWS):
                for k, value in enumerate((get_rows(val, r), get_rows(ps, r, 1), get_rows(p_s, r), get_rows(q_s, r))):
                    erow[k, i] = value
        for copy in v_copies(step):
            copy.wait()
        own_mu, own_nu = gsum[0], gsum[1]
        low, high, far = vrecv[step, 0, 0], vrecv[step, 1, 1], vrecv[step, 2, 0]
        t1, b0, b1, t2, r1, r2, e2, e3, e1, b2, z0, z1, z2 = (coef[i] for i in range(13))
        a0 = pick(own_mu, low, far, high)
        a1 = pick(acc0, own_mu, low, far) + t1 * a0
        a2 = pick(acc0, acc0, own_mu, low) + t2 * a1
        c3 = pick(low, far, high, own_nu)
        c2 = pick(far, high, own_nu, acc0) + r2 * c3
        c1 = pick(high, own_nu, acc0, acc0) + r1 * c2
        w = pick(acc0, (a0 + b0 * c1) * z0, (a1 + b1 * c2) * z1, (a2 + b2 * c3) * z2)
        y = pick((c1 + e1 * a0) * z0, (c2 + e2 * a1) * z1, (c3 + e3 * a2) * z2, acc0)
        under = jnp.where(lev == 0, acc0, w - VERT * vrecv[step, 0, 1] * inv[0])
        above = jnp.where(lev == LEVS - 1, acc0, y + VERT * vrecv[step, 1, 0] * inv[NZ - 1])

        if not last:
            for k, value in enumerate((w, y, under, above)):
                ends[k] = value

            def new_rows():
                out = []
                for i, r in enumerate(EDGE_ROWS):
                    w_r, y_r, under_r, above_r = (ends[k, r:r + 1, :] for k in range(4))
                    x = erow[0, i] + erow[2, i] * w_r + erow[3, i] * y_r
                    before = jnp.where(depth == 0, under_r, pltpu.roll(x, 1, 0))
                    after = jnp.where(depth == NZ - 1, above_r, pltpu.roll(x, NZ - 1, 0))
                    out.append(erow[1, i] - VERT * (after - before))
                return out

            rows_out(step + 1, new_rows)

        def solved(l):
            return val[l] + p_s[l] * w + q_s[l] * y

        def keep_pressure(l, p):
            if last:
                pout[l] = p
            else:
                pbuf[l, GAP:GAP + NX, :] = p

        def finish(l, carry):
            before, here = carry
            after = solved(l + 1)
            wz[l] = here
            keep_pressure(l, ps[l + 1] - VERT * (after - before))
            return here, after

        before, here = lax.fori_loop(0, NZ - 1, finish, (under, solved(0)), unroll=UNROLL)
        wz[NZ - 1] = here
        keep_pressure(NZ - 1, ps[NZ] - VERT * (above - before))


def store(*refs):
    sems = refs[-1]
    copies = [pltpu.make_async_copy(refs[i], refs[4 + i], sems.at[i]) for i in range(4)]
    for copy in copies:
        copy.start()
    for copy in copies:
        copy.wait()


def local(*blocks):
    whole = jax.ShapeDtypeStruct((NZ, NX, NY), F32)
    anywhere, hbm = pl.BlockSpec(memory_space=pl.ANY), pl.BlockSpec(memory_space=pltpu.HBM)

    def vmem(*shape):
        return pltpu.VMEM(shape, F32)

    def dma(*shape):
        return pltpu.SemaphoreType.DMA(shape)

    full, plane = (NZ, NX, NY), (NX, NY)
    blocks = pl.pallas_call(
        kernel,
        out_shape=(whole,) * 4,
        in_specs=[hbm] * 8,
        out_specs=(pl.BlockSpec(memory_space=pltpu.VMEM),) * 4,
        scratch_shapes=[
            vmem(NZ, WIDE, NY), vmem(NZ, WIDE, NY),
            vmem(NZ + 2, NX, NY),
            vmem(*full), vmem(*full), vmem(*full), vmem(*full), vmem(*full),
            vmem(*plane), vmem(*plane), vmem(*plane), vmem(*plane),
            vmem(2, *plane), vmem(2, *plane), vmem(*plane), vmem(*plane),
            vmem(4, NZ, NY),
            vmem(4, *plane), vmem(2, 4, NZ, NY),
            vmem(SUBSTEPS, 2, 2, *plane), vmem(SUBSTEPS, 2, 4, NZ, NY),
            vmem(2, *plane), vmem(2, 8, NY), vmem(2, *plane),
            vmem(3, *plane), vmem(LEVS, 3, *plane),
            vmem(5, *plane), vmem(SUBSTEPS, 3, 2, *plane), vmem(17, *plane),
            vmem(NZ + 2, NX, NY), vmem(NZ + 2, NX, NY), vmem(*full), vmem(*full),
            vmem(4, 2, *plane), vmem(*plane), vmem(2, *plane), vmem(2, 2, *plane),
            pltpu.VMEM((2 * NY, NY), BF16), vmem(*full),
            vmem(2, 12, NZ, NY), vmem(8, NZ, NY), vmem(2, *plane),
            vmem(4, 8, NZ, NY), vmem(4, *plane),
            dma(8),
            dma(4), dma(SUBSTEPS, 4), dma(3), dma(3), dma(3), dma(SUBSTEPS, 3),
            dma(4), dma(4), dma(2), dma(2),
        ],
        compiler_params=pltpu.CompilerParams(
            collective_id=0, has_side_effects=True, vmem_limit_bytes=40 * 1024 * 1024
        ),
    )(*[pltpu.with_memory_space_constraint(b, pltpu.HBM) for b in blocks])
    return pl.pallas_call(
        store,
        out_shape=(whole,) * 4,
        in_specs=[anywhere] * 4,
        out_specs=(hbm,) * 4,
        scratch_shapes=[dma(4)],
        compiler_params=pltpu.CompilerParams(vmem_limit_bytes=1024 * 1024),
        cost_estimate=pl.CostEstimate(flops=0, bytes_accessed=4_000_000, transcendentals=0),
    )(*blocks)


def solution(mesh):
    field, column = P("lev", "gx", "gy"), P("gx", "gy")
    return jax.shard_map(
        local,
        mesh=mesh,
        in_specs=(field, field, field, field, column, column, column, field),
        out_specs=(field, field, field, field),
        check_vma=False,
    )
```
